32 devices in a mesh: section: 4 (over x, core), fsdp: 2 (over y), batch: 4 (over z).
Axes of the slice: x: 2, y: 2, z: 4, core: 2. Of those that a mesh axis runs over, the one named last changes fastest.
Arguments:
- frames: bfloat16 [4, 8, 48, 1536], P(None, ('fsdp', 'batch')), may hold values from -6 to 6
- cotangent: bfloat16 [4, 8, 48, 1536], P(None, ('fsdp', 'batch')), may hold values from -6 to 6
- lengths: int32 [4, 8], P(None, ('fsdp', 'batch')), may hold values from 24 to 48
- w_in: bfloat16 [4, 1536, 3072], P('section', 'fsdp'), may hold values from -0.15625 to 0.15625
- w_out: bfloat16 [4, 1536, 1536], P('section', 'fsdp'), may hold values from -0.15625 to 0.15625
- gain_pre: float32 [4, 1536], P('section'), may hold values from 0.5 to 1.5
- gain_mid: float32 [4, 1536], P('section'), may hold values from 0.5 to 1.5
- w_depth: float32 [4, 31, 1536], P('section'), may hold values from -2 to 2
Outputs:
- input_grads: bfloat16 [4, 4, 8, 48, 1536], P('section', None, ('fsdp', 'batch'))
- grad_w_in: float32 [4, 1536, 3072], P('section', 'fsdp')
- grad_w_out: float32 [4, 1536, 1536], P('section', 'fsdp')
- grad_gain_pre: float32 [4, 1536], P('section')
- grad_gain_mid: float32 [4, 1536], P('section')
- grad_depth: float32 [4, 31, 1536], P('section')
The draws below stay inside these ranges and needn't reach their ends.
Inputs may be any that keep to these rules, and one draw needn't show every extreme that they name: `lengths`: frames at or after an utterance's length are padding.
All inputs are finite; a program needn't handle non-finite values.
Results may differ from the reference program's by a relative error of at most 0.03.
Values may be sent and summed in bfloat16 or wider, within the bound.
A program may use at most 128 MiB of HBM per device.

```python
import math
import jax
import jax.numpy as jnp
from jax import lax

D = 1536
K = 31
L = 48
MB = 4
SECTIONS = 4
UTT = 8


def set_ends(drawn, stream_key, low, largest):
    dims = drawn.shape
    index_at = [jax.random.randint(jax.random.fold_in(stream_key, axis), (), 0, dims[axis]) for axis in range(len(dims))]
    drawn = drawn.at[tuple(index_at)].set(low)
    longest = dims.index(max(dims))
    index_at[longest] = (index_at[longest] + 1) % dims[longest]
    return drawn.at[tuple(index_at)].set(largest)


def level_of(rng, extent, pieces, low, high):
    def one(position, parts):
        draws = jax.random.uniform(jax.random.fold_in(jax.random.fold_in(rng, 6), position), (parts,), jnp.float32, low / len(pieces), high / len(pieces))
        return jnp.repeat(jnp.exp(draws), extent[position] // parts).reshape((-1,) + (1,) * (len(extent) - position - 1))

    factor_of = one(*pieces[0])
    for cut in pieces[1:]:
        factor_of = factor_of * one(*cut)
    return factor_of


def scatter_about(rng, dims, deviation, reach, pieces=(), held_as=jnp.bfloat16):
    values = deviation * jax.random.normal(rng, dims, jnp.float32)
    if pieces:
        values = values * level_of(rng, dims, pieces, -0.22, 0.18)
    return jnp.clip(values, -reach, reach).astype(held_as)


def setup_inputs(seed: int = 0) -> dict:
    keys = jax.random.split(jax.random.key(seed), 9)
    return {
        "frames": scatter_about(keys[0], (MB, UTT, L, D), 1.0, 6.0, ((1, 8),)),
        "cotangent": scatter_about(keys[1], (MB, UTT, L, D), 1.0, 6.0, ((1, 8),)),
        "lengths": set_ends(jax.random.randint(keys[2], (MB, UTT), L // 2, L + 1), jax.random.fold_in(keys[2], 1), L // 2, L).astype(jnp.int32),
        "w_in": scatter_about(keys[3], (SECTIONS, D, 2 * D), D ** -0.5, 0.15625, ((0, 4), (1, 2))),
        "w_out": scatter_about(keys[4], (SECTIONS, D, D), D ** -0.5, 0.15625, ((0, 4), (1, 2))),
        "gain_pre": jnp.clip(1.0 + 0.1 * jax.random.normal(keys[5], (SECTIONS, D), jnp.float32), 0.5, 1.5),
        "gain_mid": jnp.clip(1.0 + 0.1 * jax.random.normal(keys[6], (SECTIONS, D), jnp.float32), 0.5, 1.5),
        "w_depth": scatter_about(keys[7], (SECTIONS, K, D), 8 ** -0.5, 2.0, ((0, 4),), jnp.float32),
    }


epsilon = 1e-05

def layer_norm(values):
    mean_value = lax.optimization_barrier(jnp.mean(values, axis=-1, keepdims=True))
    centred = values - mean_value
    inv_scale = lax.rsqrt(lax.optimization_barrier(jnp.mean(centred * centred, axis=-1, keepdims=True)) + epsilon)
    return (centred * inv_scale, inv_scale)

def norm_grad(upstream, normed, inv_scale):
    return (upstream - lax.optimization_barrier(jnp.mean(upstream, axis=-1, keepdims=True)) - normed * lax.optimization_barrier(jnp.mean(upstream * normed, axis=-1, keepdims=True))) * inv_scale

def project(left, right):
    batch_rows, length, inner = left.shape
    flat = jnp.dot(left.reshape(batch_rows * length, inner), right, preferred_element_type=jnp.float32)
    return flat.reshape(batch_rows, length, right.shape[1])

def project_back(left, right):
    batch_rows, length, inner = left.shape
    flat = lax.dot_general(left.reshape(batch_rows * length, inner), right, (((1,), (1,)), ((), ())), preferred_element_type=jnp.float32)
    return flat.reshape(batch_rows, length, right.shape[0])

def depthwise(values, taps):
    kernel = taps.shape[0]
    half = kernel // 2
    length = values.shape[1]
    padded = jnp.pad(values, ((0, 0), (half, half), (0, 0)))
    total = padded[:, 0:length, :] * taps[0]
    for offset in range(1, kernel):
        total = total + padded[:, offset:offset + length, :] * taps[offset]
    return total

def section_forward(frames, w_in, w_out, gain_a, gain_b, taps, padding):
    model_width = frames.shape[-1]
    source = frames.astype(jnp.float32)
    normed_in, inv_in = layer_norm(source)
    projected = (normed_in * gain_a).astype(jnp.bfloat16)
    both = project(projected, w_in)
    glu_value = both[..., :model_width]
    glu_gate = jax.nn.sigmoid(both[..., model_width:])
    gated = glu_value * glu_gate * padding
    conv_out = depthwise(gated, taps)
    normed_mid, inv_mid = layer_norm(conv_out)
    scaled_mid = normed_mid * gain_b
    swished = (scaled_mid * jax.nn.sigmoid(scaled_mid)).astype(jnp.bfloat16)
    result = (source + project(swished, w_out)).astype(jnp.bfloat16)
    return (result, (normed_in, inv_in, projected, glu_value, glu_gate, gated, normed_mid, inv_mid, scaled_mid, swished))

def section_backward(upstream, w_in, w_out, gain_a, gain_b, taps, padding, saved):
    normed_in, inv_in, projected, glu_value, glu_gate, gated, normed_mid, inv_mid, scaled_mid, swished = saved
    kernel = taps.shape[0]
    half = kernel // 2
    length = upstream.shape[1]
    swish_grad = project_back(upstream, w_out)
    sigmoid_mid = jax.nn.sigmoid(scaled_mid)
    scaled_grad = swish_grad * (sigmoid_mid + scaled_mid * sigmoid_mid * (1.0 - sigmoid_mid))
    gain_b_grad = lax.optimization_barrier(jnp.sum(scaled_grad * normed_mid, axis=(0, 1)))
    conv_grad = norm_grad(scaled_grad * gain_b, normed_mid, inv_mid)
    padded_in = jnp.pad(gated, ((0, 0), (half, half), (0, 0)))
    taps_grad = jnp.stack([lax.optimization_barrier(jnp.sum(conv_grad * padded_in[:, offset:offset + length, :], axis=(0, 1))) for offset in range(kernel)])
    padded_grad = jnp.pad(conv_grad, ((0, 0), (half, half), (0, 0)))
    gated_grad = padded_grad[:, 2 * half:2 * half + length, :] * taps[0]
    for offset in range(1, kernel):
        gated_grad = gated_grad + padded_grad[:, 2 * half - offset:2 * half - offset + length, :] * taps[offset]
    gated_grad = gated_grad * padding
    value_grad = gated_grad * glu_gate
    gate_grad = gated_grad * glu_value * glu_gate * (1.0 - glu_gate)
    proj_grad = jnp.concatenate([value_grad, gate_grad], axis=-1).astype(jnp.bfloat16)
    input_side = project_back(proj_grad, w_in)
    gain_a_grad = lax.optimization_barrier(jnp.sum(input_side * normed_in, axis=(0, 1)))
    input_grad = (upstream.astype(jnp.float32) + norm_grad(input_side * gain_a, normed_in, inv_in)).astype(jnp.bfloat16)
    return (input_grad, proj_grad, (gain_a_grad, gain_b_grad, taps_grad))

def by_utterance(values, micro_count, utterances):
    length = values.shape[1]
    last_dim = values.shape[2]
    grouped = values.reshape(micro_count, utterances, length, last_dim).transpose(1, 0, 2, 3)
    return grouped.reshape(utterances, micro_count * length, last_dim)

def device_terms(lefts, rights):

    def accumulate(total, pair):
        term = lax.dot_general(pair[0], pair[1], (((0,), (0,)), ((), ())), preferred_element_type=jnp.float32)
        return (total + lax.optimization_barrier(term.astype(jnp.bfloat16)).astype(jnp.float32), None)
    start = jnp.zeros((lefts.shape[2], rights.shape[2]), jnp.float32)
    total, unused = lax.scan(accumulate, start, (lefts, rights))
    return total

def reference(frames, cotangent, lengths, w_in, w_out, gain_pre, gain_mid, w_depth):
    micro_count, utterances, frames_len, model_width = frames.shape
    section_count = w_in.shape[0]
    batch_rows = micro_count * utterances
    positions = jnp.arange(frames_len, dtype=jnp.int32)
    padding = (positions[None, None, :] < lengths[:, :, None]).astype(jnp.float32).reshape(batch_rows, frames_len, 1)
    scale = 1.0 / math.sqrt(micro_count * utterances * frames_len)
    current = frames.reshape(batch_rows, frames_len, model_width)
    section_inputs = []
    for section_index in range(section_count):
        section_inputs.append(current)
        current, unused = section_forward(current, w_in[section_index], w_out[section_index], gain_pre[section_index], gain_mid[section_index], w_depth[section_index], padding)
    upstream = cotangent.reshape(batch_rows, frames_len, model_width)
    grads_in = [None] * section_count
    grads_proj_in = [None] * section_count
    grads_proj_out = [None] * section_count
    grads_pre = [None] * section_count
    grads_mid = [None] * section_count
    grads_taps = [None] * section_count
    for section_index in reversed(range(section_count)):
        params = (w_in[section_index], w_out[section_index], gain_pre[section_index], gain_mid[section_index], w_depth[section_index])
        unused, saved = section_forward(section_inputs[section_index], params[0], params[1], params[2], params[3], params[4], padding)
        input_grad, proj_grad, minor_grads = section_backward(upstream, params[0], params[1], params[2], params[3], params[4], padding, saved)
        grads_proj_in[section_index] = scale * device_terms(by_utterance(saved[2], micro_count, utterances), by_utterance(proj_grad, micro_count, utterances))
        grads_proj_out[section_index] = scale * device_terms(by_utterance(saved[9], micro_count, utterances), by_utterance(upstream, micro_count, utterances))
        grads_pre[section_index] = scale * minor_grads[0]
        grads_mid[section_index] = scale * minor_grads[1]
        grads_taps[section_index] = scale * minor_grads[2]
        grads_in[section_index] = input_grad.reshape(micro_count, utterances, frames_len, model_width)
        upstream = input_grad
    return (jnp.stack(grads_in), jnp.stack(grads_proj_in), jnp.stack(grads_proj_out), jnp.stack(grads_pre), jnp.stack(grads_mid), jnp.stack(grads_taps))
```

```python
import functools
import math

import jax
import jax.numpy as jnp
from jax import lax
from jax.experimental import pallas as pl
from jax.experimental.pallas import tpu as pltpu
from jax.sharding import PartitionSpec as P

epsilon = 1e-05
GROUP = 2


def from_behind(x, axis, by):
    peers = lax.axis_size(axis)
    pairs = [(i, i + by) for i in range(peers) if 0 <= i + by < peers]
    return lax.ppermute(x, axis, pairs)


def layer_norm(values):
    mean_value = jnp.mean(values, axis=-1, keepdims=True)
    centred = values - mean_value
    inv_scale = lax.rsqrt(jnp.mean(centred * centred, axis=-1, keepdims=True) + epsilon)
    return (centred * inv_scale, inv_scale)


def norm_grad(upstream, normed, inv_scale):
    return (
        upstream
        - jnp.mean(upstream, axis=-1, keepdims=True)
        - normed * jnp.mean(upstream * normed, axis=-1, keepdims=True)
    ) * inv_scale


def project(left, right):
    batch_rows, length, inner = left.shape
    flat = jnp.dot(
        left.reshape(batch_rows * length, inner), right, preferred_element_type=jnp.float32
    )
    return flat.reshape(batch_rows, length, right.shape[1])


def project_back(left, right):
    batch_rows, length, inner = left.shape
    flat = lax.dot_general(
        left.reshape(batch_rows * length, inner),
        right,
        (((1,), (1,)), ((), ())),
        preferred_element_type=jnp.float32,
    )
    return flat.reshape(batch_rows, length, right.shape[0])


def depthwise(values, taps):
    kernel = taps.shape[0]
    half = kernel // 2
    length = values.shape[1]
    padded = jnp.pad(values, ((0, 0), (half, half), (0, 0)))
    total = padded[:, 0:length, :] * taps[0]
    for offset in range(1, kernel):
        total = total + padded[:, offset : offset + length, :] * taps[offset]
    return total


def section_forward(frames, w_in, w_out, gain_a, gain_b, taps, padding):
    model_width = frames.shape[-1]
    source = frames.astype(jnp.float32)
    normed_in, inv_in = layer_norm(source)
    projected = (normed_in * gain_a).astype(jnp.bfloat16)
    both = project(projected, w_in)
    glu_value = both[..., :model_width]
    glu_gate = jax.nn.sigmoid(both[..., model_width:])
    gated = glu_value * glu_gate * padding
    conv_out = depthwise(gated, taps)
    normed_mid, inv_mid = layer_norm(conv_out)
    scaled_mid = normed_mid * gain_b
    swished = (scaled_mid * jax.nn.sigmoid(scaled_mid)).astype(jnp.bfloat16)
    result = (source + project(swished, w_out)).astype(jnp.bfloat16)
    return (
        result,
        (
            normed_in,
            inv_in,
            projected,
            glu_value,
            glu_gate,
            gated,
            normed_mid,
            inv_mid,
            scaled_mid,
            swished,
        ),
    )


def section_backward(upstream, w_in, w_out, gain_a, gain_b, taps, padding, saved):
    (
        normed_in,
        inv_in,
        projected,
        glu_value,
        glu_gate,
        gated,
        normed_mid,
        inv_mid,
        scaled_mid,
        swished,
    ) = saved
    kernel = taps.shape[0]
    half = kernel // 2
    length = upstream.shape[1]
    swish_grad = project_back(upstream, w_out)
    sigmoid_mid = jax.nn.sigmoid(scaled_mid)
    scaled_grad = swish_grad * (sigmoid_mid + scaled_mid * sigmoid_mid * (1.0 - sigmoid_mid))
    gain_b_grad = jnp.sum(scaled_grad * normed_mid, axis=(0, 1))
    conv_grad = norm_grad(scaled_grad * gain_b, normed_mid, inv_mid)
    padded_in = jnp.pad(gated, ((0, 0), (half, half), (0, 0)))
    taps_grad = jnp.stack(
        [
            jnp.sum(conv_grad * padded_in[:, offset : offset + length, :], axis=(0, 1))
            for offset in range(kernel)
        ]
    )
    padded_grad = jnp.pad(conv_grad, ((0, 0), (half, half), (0, 0)))
    gated_grad = padded_grad[:, 2 * half : 2 * half + length, :] * taps[0]
    for offset in range(1, kernel):
        gated_grad = (
            gated_grad
            + padded_grad[:, 2 * half - offset : 2 * half - offset + length, :] * taps[offset]
        )
    gated_grad = gated_grad * padding
    value_grad = gated_grad * glu_gate
    gate_grad = gated_grad * glu_value * glu_gate * (1.0 - glu_gate)
    proj_grad = jnp.concatenate([value_grad, gate_grad], axis=-1).astype(jnp.bfloat16)
    input_side = project_back(proj_grad, w_in)
    gain_a_grad = jnp.sum(input_side * normed_in, axis=(0, 1))
    input_grad = (
        upstream.astype(jnp.float32) + norm_grad(input_side * gain_a, normed_in, inv_in)
    ).astype(jnp.bfloat16)
    return (input_grad, proj_grad, (gain_a_grad, gain_b_grad, taps_grad))


def saved_zeros(micro_count, frames_len, model_width):
    wide = (micro_count, 1, frames_len, model_width)
    narrow = (micro_count, 1, frames_len, 1)
    return (
        jnp.zeros(wide, jnp.float32),
        jnp.zeros(narrow, jnp.float32),
        jnp.zeros(wide, jnp.bfloat16),
        jnp.zeros(wide, jnp.float32),
        jnp.zeros(wide, jnp.float32),
        jnp.zeros(wide, jnp.float32),
        jnp.zeros(wide, jnp.float32),
        jnp.zeros(narrow, jnp.float32),
        jnp.zeros(wide, jnp.float32),
        jnp.zeros(wide, jnp.bfloat16),
    )


def put_slot(buffers, values, micro_slot):
    return jax.tree.map(
        lambda buffer, value: lax.dynamic_update_index_in_dim(buffer, value, micro_slot, 0),
        buffers,
        values,
    )


def take_slot(buffers, micro_slot):
    return jax.tree.map(
        lambda buffer: lax.dynamic_index_in_dim(buffer, micro_slot, 0, keepdims=False), buffers
    )


def local(frames, cotangent, lengths, w_in, w_out, gain_pre, gain_mid, w_depth):
    section_count = lax.axis_size("section")
    section_index = lax.axis_index("section")
    micro_count = frames.shape[0]
    frames_len = frames.shape[2]
    model_width = frames.shape[3]
    moments = micro_count + section_count - 1
    scale = 1.0 / math.sqrt(
        micro_count * frames_len * lax.axis_size("fsdp") * lax.axis_size("batch")
    )
    w_in_full, w_out_full = (
        lax.all_gather(w_in[0], "fsdp", axis=0, tiled=True),
        lax.all_gather(w_out[0], "fsdp", axis=0, tiled=True),
    )
    gain_a = gain_pre[0]
    gain_b = gain_mid[0]
    taps = w_depth[0]
    positions = jnp.arange(frames_len, dtype=jnp.int32)

    def frame_padding(micro_slot):
        return (positions < lengths[micro_slot, 0]).astype(jnp.float32).reshape(1, frames_len, 1)

    stored = saved_zeros(micro_count, frames_len, model_width)
    blank = jnp.zeros((1, frames_len, model_width), jnp.bfloat16)
    outgoing = blank
    for moment in range(moments):
        if moment > 0:
            incoming = from_behind(outgoing, "section", 1)
        else:
            incoming = blank
        if moment < micro_count:
            section_input = jnp.where(section_index == 0, frames[moment], incoming)
        else:
            section_input = incoming
        micro_index = moment - section_index
        active = (micro_index >= 0) & (micro_index < micro_count)
        micro_slot = jnp.clip(micro_index, 0, micro_count - 1)

        def advance(operands, micro_slot=micro_slot):
            current, buffers = operands
            result, saved = section_forward(
                current, w_in_full, w_out_full, gain_a, gain_b, taps, frame_padding(micro_slot)
            )
            return (result, put_slot(buffers, saved, micro_slot))

        def bypass(operands):
            return (jnp.zeros_like(operands[0]), operands[1])

        outgoing, stored = lax.cond(active, advance, bypass, (section_input, stored))
    row_buffers = (
        jnp.zeros((micro_count, frames_len, model_width), jnp.bfloat16),
        jnp.zeros((micro_count, frames_len, 2 * model_width), jnp.bfloat16),
        jnp.zeros((micro_count, frames_len, model_width), jnp.bfloat16),
        jnp.zeros((micro_count, frames_len, model_width), jnp.bfloat16),
        jnp.zeros((micro_count, frames_len, model_width), jnp.bfloat16),
    )
    small_sums = (
        jnp.zeros((model_width,), jnp.float32),
        jnp.zeros((model_width,), jnp.float32),
        jnp.zeros(taps.shape, jnp.float32),
    )
    returning = blank
    for moment in range(moments):
        if moment > 0:
            incoming = from_behind(returning, "section", -1)
        else:
            incoming = blank
        if moment < micro_count:
            upstream = jnp.where(section_index == section_count - 1, cotangent[moment], incoming)
        else:
            upstream = incoming
        micro_index = moment - (section_count - 1 - section_index)
        active = (micro_index >= 0) & (micro_index < micro_count)
        micro_slot = jnp.clip(micro_index, 0, micro_count - 1)

        def retreat(operands, micro_slot=micro_slot):
            current, buffers, totals = operands
            padding = frame_padding(micro_slot)
            saved = take_slot(stored, micro_slot)
            input_grad, proj_grad, minor_grads = section_backward(
                current, w_in_full, w_out_full, gain_a, gain_b, taps, padding, saved
            )
            row_values = (saved[2][0], proj_grad[0], saved[9][0], current[0], input_grad[0])
            buffers = put_slot(buffers, row_values, micro_slot)
            totals = tuple((total + extra for total, extra in zip(totals, minor_grads)))
            return (input_grad, buffers, totals)

        def hold(operands):
            return (jnp.zeros_like(operands[0]), operands[1], operands[2])

        returning, row_buffers, small_sums = lax.cond(
            active, retreat, hold, (upstream, row_buffers, small_sums)
        )
    total_rows = micro_count * frames_len
    proj_rows = row_buffers[0].reshape(total_rows, model_width)
    grad_rows = row_buffers[1].reshape(total_rows, 2 * model_width)
    swish_rows = row_buffers[2].reshape(total_rows, model_width)
    upstream_rows = row_buffers[3].reshape(total_rows, model_width)
    term_in = lax.dot_general(
        proj_rows, grad_rows, (((0,), (0,)), ((), ())), preferred_element_type=jnp.float32
    )
    term_out = lax.dot_general(
        swish_rows, upstream_rows, (((0,), (0,)), ((), ())), preferred_element_type=jnp.float32
    )
    rounded_in = lax.optimization_barrier(term_in.astype(jnp.bfloat16)).astype(jnp.float32)
    rounded_out = lax.optimization_barrier(term_out.astype(jnp.bfloat16)).astype(jnp.float32)
    shares = (
        lax.psum_scatter(
            rounded_in.astype(jnp.bfloat16), "fsdp", scatter_dimension=0, tiled=True
        ).astype(jnp.float32),
        lax.psum_scatter(
            rounded_out.astype(jnp.bfloat16), "fsdp", scatter_dimension=0, tiled=True
        ).astype(jnp.float32),
    )
    grad_in, grad_out = (
        lax.psum(shares[0].astype(jnp.bfloat16), "batch").astype(jnp.float32),
        lax.psum(shares[1].astype(jnp.bfloat16), "batch").astype(jnp.float32),
    )
    small_total = lax.psum((small_sums[0], small_sums[1], small_sums[2]), ("fsdp", "batch"))
    input_grads = row_buffers[4].reshape(1, micro_count, 1, frames_len, model_width)
    return (
        input_grads,
        (scale * grad_in)[None],
        (scale * grad_out)[None],
        (scale * small_total[0])[None],
        (scale * small_total[1])[None],
        (scale * small_total[2])[None],
    )


TILE = 256
LANES = 128
EDGE = 16


def pipeline_kernel(
    dims,
    frames,
    cotangent,
    pad,
    w_in,
    w_out,
    gain_pre,
    gain_mid,
    taps,
    ig,
    total,
    small_total,
    win,
    wout,
    xin,
    xout,
    nin,
    inv_in,
    proj,
    val,
    gate,
    gpad,
    nmid,
    inv_mid,
    sw,
    mid,
    cpad,
    tg,
    lp,
    ls,
    right,
    part,
    arrived,
    small,
    small_y,
    small_sum,
    small_a,
    small_b,
    w_ys,
    w_yr,
    w_zs,
    w_zr,
    w_loc,
    f_s,
    f_r,
    b_s,
    b_r,
    yp_s,
    yp_r,
    ysw_s,
    ysw_r,
    yu_s,
    yu_r,
    yg_s,
    yg_r,
    sy_s,
    sy_r,
    a_s,
    a_r,
    c_s,
    c_r,
    t_s,
    t_r,
):
    steps, group, length, width, kernel = dims
    rows = group * length
    tiles = width // TILE
    half = width // 2
    f32, bf16 = jnp.float32, jnp.bfloat16
    sections = lax.axis_size("section")
    sec = lax.axis_index("section")
    fs = lax.axis_index("fsdp")
    ba = lax.axis_index("batch")
    other = 1 - fs
    mate = ba + 1 - 2 * lax.rem(ba, 2)
    parity = lax.rem(ba, 2)
    edge = (ba == 0) | (ba == 3)
    inner = jnp.where(ba == 0, 1, 2)
    outer = jnp.where(ba == 1, 0, 3)
    opposite = 3 - ba

    def remote(src, dst, send, recv, **where):
        return pltpu.make_async_remote_copy(
            src_ref=src,
            dst_ref=dst,
            send_sem=send,
            recv_sem=recv,
            device_id=where,
            device_id_type=pl.DeviceIdType.MESH,
        )

    def tile(j, base=0):
        return pl.ds(pl.multiple_of(base + j * TILE, TILE), TILE)

    barrier = pltpu.get_barrier_semaphore()
    for where in (
        {"section": lax.rem(sec + 1, sections)},
        {"section": lax.rem(sec + sections - 1, sections)},
        {"fsdp": other},
        {"batch": lax.rem(ba + 1, 4)},
        {"batch": lax.rem(ba + 3, 4)},
    ):
        pl.semaphore_signal(barrier, inc=1, device_id=where, device_id_type=pl.DeviceIdType.MESH)
    pl.semaphore_wait(barrier, 5)

    pieces = []
    in_rows, out_rows = half // 8, half // 4
    for i in range(6):
        if i < 4:
            pieces.append((w_in, win, in_rows, (2 * i, 2 * i)))
        else:
            pieces.append((w_out, wout, out_rows, (2 * (i - 4), 2 * (i - 4))))

    def span(size, first, which, owner=None):
        begin = (first + which) * size
        if owner is not None:
            begin = owner * half + begin
        return pl.ds(pl.multiple_of(begin, 16), size)

    def over_y(i):
        src, dst, size, (first, _) = pieces[i]
        return remote(
            src.at[span(size, first, parity)],
            dst.at[span(size, first, parity, fs)],
            w_ys.at[i],
            w_yr.at[i],
            fsdp=other,
        )

    def over_z(i):
        _, dst, size, (first, _) = pieces[i]
        block = dst.at[span(size, first, parity, other)]
        return remote(block, block, w_zs.at[i], w_zr.at[i], batch=mate)

    for i in range(6):
        over_y(i).start()
    own = pl.ds(pl.multiple_of(fs * half, 16), half)
    own_in = pltpu.make_async_copy(w_in, win.at[own], w_loc.at[0])
    own_out = pltpu.make_async_copy(w_out, wout.at[own], w_loc.at[1])
    own_in.start()
    own_out.start()

    gpad[...] = jnp.zeros_like(gpad)
    cpad[...] = jnp.zeros_like(cpad)
    tg[...] = jnp.zeros_like(tg)
    small[...] = jnp.zeros_like(small)

    for i in range(6):
        over_y(i).wait_recv()
        over_z(i).start()
    own_in.wait()
    own_out.wait()
    for i in range(6):
        over_z(i).wait_recv()

    mine = pl.ds(pl.multiple_of(fs * half, LANES), half)
    theirs = pl.ds(pl.multiple_of(other * half, LANES), half)

    def send_forward(s):
        return remote(xout.at[s], xin.at[s], f_s.at[s], f_r.at[s], section=lax.rem(sec + 1, sections))

    def send_backward(s):
        return remote(
            ig.at[s],
            right.at[s, :, pl.ds(2 * width, width)],
            b_s.at[s],
            b_r.at[s],
            section=lax.rem(sec + sections - 1, sections),
        )

    def send_proj(s):
        return remote(proj.at[s, :, theirs], lp.at[steps + s], yp_s.at[s], yp_r.at[s], fsdp=other)

    def send_sw(s):
        return remote(sw.at[s, :, theirs], ls.at[steps + s], ysw_s.at[s], ysw_r.at[s], fsdp=other)

    def send_up(s):
        cols = pl.ds(2 * width, width)
        return remote(
            right.at[s, :, cols], right.at[steps + s, :, cols], yu_s.at[s], yu_r.at[s], fsdp=other
        )

    def send_grad(s):
        cols = pl.ds(0, 2 * width)
        return remote(
            right.at[s, :, cols], right.at[steps + s, :, cols], yg_s.at[s], yg_r.at[s], fsdp=other
        )

    def norm_stats(values):
        mean_value = jnp.sum(values, axis=-1, keepdims=True) * (1.0 / width)
        centred = values - mean_value
        inv = lax.rsqrt(jnp.sum(centred * centred, axis=-1, keepdims=True) * (1.0 / width) + epsilon)
        return centred * inv, inv

    def forward(s, carry):
        @pl.when(sec == 0)
        def _():
            xin[s] = frames[s]

        @pl.when(sec > 0)
        def _():
            send_forward(s).wait_recv()

        normed, inv = norm_stats(xin[s].astype(f32))
        nin[s] = normed
        inv_in[s] = inv
        proj[s] = (normed * gain_pre[...]).astype(bf16)
        send_proj(s).start()
        lp[s] = proj[s, :, mine]

        def first(j, carry):
            left = proj[s]
            v = jnp.dot(left, win[:, tile(j)], preferred_element_type=f32)
            g = jax.nn.sigmoid(
                jnp.dot(left, win[:, tile(j, width)], preferred_element_type=f32)
            )
            val[s, :, tile(j)] = v
            gate[s, :, tile(j)] = g
            gated = v * g * pad[s]
            for m in range(group):
                gpad[s * group + m, EDGE : EDGE + length, tile(j)] = gated[
                    m * length : (m + 1) * length
                ]
            for m in range(group):
                for c in range(TILE // LANES):
                    cols = pl.ds(pl.multiple_of(j * TILE + c * LANES, LANES), LANES)
                    acc = jnp.zeros((length, LANES), f32)
                    for b in range(8):
                        rolled = gpad[s * group + m, b : b + length + 24, cols]
                        for a in range(4):
                            k = 8 * a + b - 1
                            if 0 <= k < kernel:
                                acc = acc + rolled[8 * a : 8 * a + length] * taps[k : k + 1, cols]
                    mid[m * length : (m + 1) * length, cols] = acc
            return carry

        lax.fori_loop(0, tiles, first, 0)
        normed2, inv2 = norm_stats(mid[...])
        nmid[s] = normed2
        inv_mid[s] = inv2
        scaled = normed2 * gain_mid[...]
        sw[s] = (scaled * jax.nn.sigmoid(scaled)).astype(bf16)
        send_sw(s).start()
        ls[s] = sw[s, :, mine]

        @pl.when(sec < sections - 1)
        def _():
            def second(j, carry):
                out = jnp.dot(sw[s], wout[:, tile(j)], preferred_element_type=f32)
                xout[s, :, tile(j)] = (xin[s, :, tile(j)].astype(f32) + out).astype(bf16)
                return carry

            lax.fori_loop(0, tiles, second, 0)
            send_forward(s).start()

        return carry

    lax.fori_loop(0, steps, forward, 0)

    nt = (((1,), (1,)), ((), ()))

    def backward(s, carry):
        @pl.when(sec == sections - 1)
        def _():
            right[s, :, pl.ds(2 * width, width)] = cotangent[s]

        @pl.when(sec < sections - 1)
        def _():
            send_backward(s).wait_recv()

        send_up(s).start()
        zero = jnp.zeros((rows, 1), f32)

        def first(j, sums):
            up = right[s, :, pl.ds(2 * width, width)]
            sg = lax.dot_general(up, wout[tile(j), :], nt, preferred_element_type=f32)
            nm = nmid[s, :, tile(j)]
            gb = gain_mid[:, tile(j)]
            scaled = nm * gb
            sig = jax.nn.sigmoid(scaled)
            scg = sg * (sig + scaled * sig * (1.0 - sig))
            small[1:2, tile(j)] += jnp.sum(scg * nm, axis=0, keepdims=True)
            z = scg * gb
            mid[:, tile(j)] = z
            return (
                sums[0] + jnp.sum(z, axis=-1, keepdims=True),
                sums[1] + jnp.sum(z * nm, axis=-1, keepdims=True),
            )

        s1, s2 = lax.fori_loop(0, tiles, first, (zero, zero))
        s1 = s1 * (1.0 / width)
        s2 = s2 * (1.0 / width)

        def second(j, carry):
            cols = pl.ds(pl.multiple_of(j * LANES, LANES), LANES)
            gate_cols = pl.ds(pl.multiple_of(width + j * LANES, LANES), LANES)
            cg_all = (mid[:, cols] - s1 - nmid[s, :, cols] * s2) * inv_mid[s]
            for m in range(group):
                span_m = slice(m * length, (m + 1) * length)
                cg = cg_all[span_m]
                cpad[m, EDGE : EDGE + length, :] = cg
                for b in range(8):
                    rolled = gpad[s * group + m, b : b + length + 24, cols]
                    for a in range(4):
                        k = 8 * a + b - 1
                        if 0 <= k < kernel:
                            term = cg * rolled[8 * a : 8 * a + length]
                            tg[k, :, cols] += jnp.sum(term.reshape(length // 8, 8, LANES), axis=0)
                acc = jnp.zeros((length, LANES), f32)
                for b in range(8):
                    rolled = cpad[m, b : b + length + 24, :]
                    for a in range(4):
                        k = kernel - 1 - (8 * a + b - 1)
                        if 0 <= k < kernel:
                            acc = acc + rolled[8 * a : 8 * a + length] * taps[k : k + 1, cols]
                acc = acc * pad[s, span_m]
                g = gate[s, span_m, cols]
                vg = acc * g
                right[s, span_m, cols] = vg.astype(bf16)
                right[s, span_m, gate_cols] = (
                    acc * val[s, span_m, cols] * g * (1.0 - g)
                ).astype(bf16)
            return carry

        lax.fori_loop(0, width // LANES, second, 0)
        send_grad(s).start()

        def third(j, sums):
            pg = right[s, :, pl.ds(0, 2 * width)]
            ins = lax.dot_general(pg, win[tile(j), :], nt, preferred_element_type=f32)
            nv = nin[s, :, tile(j)]
            small[0:1, tile(j)] += jnp.sum(ins * nv, axis=0, keepdims=True)
            z = ins * gain_pre[:, tile(j)]
            mid[:, tile(j)] = z
            return (
                sums[0] + jnp.sum(z, axis=-1, keepdims=True),
                sums[1] + jnp.sum(z * nv, axis=-1, keepdims=True),
            )

        m1, m2 = lax.fori_loop(0, tiles, third, (zero, zero))
        m1 = m1 * (1.0 / width)
        m2 = m2 * (1.0 / width)
        up = right[s, :, pl.ds(2 * width, width)].astype(f32)
        ig[s] = (up + (mid[...] - m1 - nin[s] * m2) * inv_in[s]).astype(bf16)

        @pl.when(sec > 0)
        def _():
            send_backward(s).start()

        return carry

    lax.fori_loop(0, steps, backward, 0)

    small[8 : 8 + kernel] = jnp.sum(tg[...], axis=1)
    swap = remote(small, small_y, sy_s, sy_r, fsdp=other)
    swap.start()

    def arrivals(s, carry):
        send_proj(s).wait_recv()
        send_sw(s).wait_recv()
        send_up(s).wait_recv()
        send_grad(s).wait_recv()
        return carry

    lax.fori_loop(0, steps, arrivals, 0)
    swap.wait_recv()
    small_sum[...] = small[...] + small_y[...]

    chunks = 3 * tiles

    def chunk_to_inner(c):
        return remote(
            part.at[:, tile(c)], arrived.at[:, tile(c)], a_s.at[c], a_r.at[c], batch=inner
        )

    def chunk_across(c):
        return remote(
            part.at[:, tile(c)], total.at[:, tile(c)], c_s.at[c], c_r.at[c], batch=opposite
        )

    def chunk_to_outer(c):
        return remote(
            total.at[:, tile(c)], total.at[:, tile(c)], t_s.at[c], t_r.at[c], batch=outer
        )

    small_to_inner = remote(small_sum, small_a, a_s.at[chunks], a_r.at[chunks], batch=inner)
    small_across = remote(small_sum, small_b, c_s.at[chunks], c_r.at[chunks], batch=opposite)
    small_to_outer = remote(small_total, small_total, t_s.at[chunks], t_r.at[chunks], batch=outer)

    tn = (((0,), (0,)), ((), ()))

    def terms(left_ref, first_chunk, count):
        def one(c, carry):
            left = left_ref[...].reshape(2 * steps * rows, half)
            block = right[:, :, tile(c)].reshape(2 * steps * rows, TILE)
            part[:, tile(c)] = lax.dot_general(
                left, block, tn, preferred_element_type=f32
            ).astype(bf16)

            @pl.when(edge)
            def _():
                chunk_to_inner(c).start()

            return carry

        lax.fori_loop(first_chunk, first_chunk + count, one, 0)

    @pl.when(edge)
    def _():
        small_to_inner.start()

    terms(lp, 0, 2 * tiles)
    terms(ls, 2 * tiles, tiles)

    @pl.when(jnp.logical_not(edge))
    def _():
        small_to_inner.wait_recv()
        small_sum[...] = small_sum[...] + small_a[...]
        small_across.start()

        def finish(c):
            chunk_across(c).wait_recv()
            chunk_across(c).wait_send()
            total[:, tile(c)] = (
                part[:, tile(c)].astype(f32) + total[:, tile(c)].astype(f32)
            ).astype(bf16)
            chunk_to_outer(c).start()

        def meet(c, carry):
            chunk_to_inner(c).wait_recv()
            part[:, tile(c)] = (
                part[:, tile(c)].astype(f32) + arrived[:, tile(c)].astype(f32)
            ).astype(bf16)
            chunk_across(c).start()

            @pl.when(c > 0)
            def _():
                finish(c - 1)

            return carry

        lax.fori_loop(0, chunks, meet, 0)
        finish(chunks - 1)
        small_across.wait_recv()
        small_across.wait_send()
        small_total[...] = small_sum[...] + small_b[...]
        small_to_outer.start()

        def sent(c, carry):
            chunk_to_outer(c).wait_send()
            return carry

        lax.fori_loop(0, chunks, sent, 0)
        small_to_outer.wait_send()

    @pl.when(edge)
    def _():
        def done(c, carry):
            chunk_to_inner(c).wait_send()
            chunk_to_outer(c).wait_recv()
            return carry

        lax.fori_loop(0, chunks, done, 0)
        small_to_inner.wait_send()
        small_to_outer.wait_recv()

    for i in range(6):
        over_y(i).wait_send()
        over_z(i).wait_send()
    swap.wait_send()

    def drained(s, carry):
        send_proj(s).wait_send()
        send_sw(s).wait_send()
        send_up(s).wait_send()
        send_grad(s).wait_send()

        @pl.when(sec < sections - 1)
        def _():
            send_forward(s).wait_send()

        @pl.when(sec > 0)
        def _():
            send_backward(s).wait_send()

        return carry

    lax.fori_loop(0, steps, drained, 0)


def fused(frames, cotangent, lengths, w_in, w_out, gain_pre, gain_mid, w_depth):
    micro_count, _, length, width = frames.shape
    kernel = w_depth.shape[1]
    group = GROUP
    steps = micro_count // group
    rows = group * length
    half = w_in.shape[1]
    scale = 1.0 / math.sqrt(micro_count * length * lax.axis_size("fsdp") * lax.axis_size("batch"))
    positions = jnp.arange(length, dtype=jnp.int32)
    pad = (positions[None, :] < lengths).astype(jnp.float32).reshape(steps, rows, 1)
    f32, bf16 = jnp.float32, jnp.bfloat16
    chunks = 3 * (width // TILE)
    small_rows = 8 + -(-kernel // 8) * 8
    vmem = pl.BlockSpec(memory_space=pltpu.VMEM)
    hbm = pl.BlockSpec(memory_space=pl.ANY)

    def buf(*shape, dtype=f32):
        return pltpu.VMEM(shape, dtype)

    def sem(*shape):
        return pltpu.SemaphoreType.DMA(shape)

    ig, total, small = pl.pallas_call(
        functools.partial(pipeline_kernel, (steps, group, length, width, kernel)),
        out_shape=(
            jax.ShapeDtypeStruct((steps, rows, width), bf16),
            jax.ShapeDtypeStruct((half, 3 * width), bf16),
            jax.ShapeDtypeStruct((small_rows, width), f32),
        ),
        in_specs=[vmem, vmem, vmem, hbm, hbm, vmem, vmem, vmem],
        out_specs=(vmem, vmem, vmem),
        scratch_shapes=[
            buf(width, 2 * width, dtype=bf16),
            buf(width, width, dtype=bf16),
            buf(steps, rows, width, dtype=bf16),
            buf(steps, rows, width, dtype=bf16),
            buf(steps, rows, width),
            buf(steps, rows, 1),
            buf(steps, rows, width, dtype=bf16),
            buf(steps, rows, width),
            buf(steps, rows, width),
            buf(micro_count, length + 2 * EDGE, width),
            buf(steps, rows, width),
            buf(steps, rows, 1),
            buf(steps, rows, width, dtype=bf16),
            buf(rows, width),
            buf(group, length + 2 * EDGE, LANES),
            buf(kernel, 8, width),
            buf(2 * steps, rows, half, dtype=bf16),
            buf(2 * steps, rows, half, dtype=bf16),
            buf(2 * steps, rows, 3 * width, dtype=bf16),
            buf(half, 3 * width, dtype=bf16),
            buf(half, 3 * width, dtype=bf16),
            buf(small_rows, width),
            buf(small_rows, width),
            buf(small_rows, width),
            buf(small_rows, width),
            buf(small_rows, width),
            sem(6),
            sem(6),
            sem(6),
            sem(6),
            sem(2),
            *[sem(steps) for _ in range(12)],
            pltpu.SemaphoreType.DMA,
            pltpu.SemaphoreType.DMA,
            *[sem(chunks + 1) for _ in range(6)],
        ],
        compiler_params=pltpu.CompilerParams(
            collective_id=0, has_side_effects=True, vmem_limit_bytes=62 * 1024 * 1024
        ),
    )(
        frames.reshape(steps, rows, width),
        cotangent.reshape(steps, rows, width),
        pad,
        w_in[0],
        w_out[0],
        gain_pre,
        gain_mid,
        w_depth[0],
    )
    return (
        ig.reshape(1, micro_count, 1, length, width),
        (scale * total[:, : 2 * width].astype(f32))[None],
        (scale * total[:, 2 * width :].astype(f32))[None],
        (scale * small[0])[None],
        (scale * small[1])[None],
        (scale * small[8 : 8 + kernel])[None],
    )


def solution(mesh):
    in_specs = (
        P(None, ("fsdp", "batch"), None, None),
        P(None, ("fsdp", "batch"), None, None),
        P(None, ("fsdp", "batch")),
        P("section", "fsdp", None),
        P("section", "fsdp", None),
        P("section", None),
        P("section", None),
        P("section", None, None),
    )
    out_specs = (
        P("section", None, ("fsdp", "batch"), None, None),
        P("section", "fsdp", None),
        P("section", "fsdp", None),
        P("section", None),
        P("section", None),
        P("section", None, None),
    )
    paired = mesh.shape["fsdp"] == 2 and mesh.shape["batch"] == 4
    body = fused if paired else local
    return jax.shard_map(body, mesh=mesh, in_specs=in_specs, out_specs=out_specs, check_vma=False)
```

```python
import functools
import math

import jax
import jax.numpy as jnp
from jax import lax
from jax.experimental import pallas as pl
from jax.experimental.pallas import tpu as pltpu
from jax.sharding import PartitionSpec as P

epsilon = 1e-05
GROUP = 2


def from_behind(x, axis, by):
    peers = lax.axis_size(axis)
    pairs = [(i, i + by) for i in range(peers) if 0 <= i + by < peers]
    return lax.ppermute(x, axis, pairs)


def layer_norm(values):
    mean_value = jnp.mean(values, axis=-1, keepdims=True)
    centred = values - mean_value
    inv_scale = lax.rsqrt(jnp.mean(centred * centred, axis=-1, keepdims=True) + epsilon)
    return (centred * inv_scale, inv_scale)


def norm_grad(upstream, normed, inv_scale):
    return (
        upstream
        - jnp.mean(upstream, axis=-1, keepdims=True)
        - normed * jnp.mean(upstream * normed, axis=-1, keepdims=True)
    ) * inv_scale


def project(left, right):
    batch_rows, length, inner = left.shape
    flat = jnp.dot(
        left.reshape(batch_rows * length, inner), right, preferred_element_type=jnp.float32
    )
    return flat.reshape(batch_rows, length, right.shape[1])


def project_back(left, right):
    batch_rows, length, inner = left.shape
    flat = lax.dot_general(
        left.reshape(batch_rows * length, inner),
        right,
        (((1,), (1,)), ((), ())),
        preferred_element_type=jnp.float32,
    )
    return flat.reshape(batch_rows, length, right.shape[0])


def depthwise(values, taps):
    kernel = taps.shape[0]
    half = kernel // 2
    length = values.shape[1]
    padded = jnp.pad(values, ((0, 0), (half, half), (0, 0)))
    total = padded[:, 0:length, :] * taps[0]
    for offset in range(1, kernel):
        total = total + padded[:, offset : offset + length, :] * taps[offset]
    return total


def section_forward(frames, w_in, w_out, gain_a, gain_b, taps, padding):
    model_width = frames.shape[-1]
    source = frames.astype(jnp.float32)
    normed_in, inv_in = layer_norm(source)
    projected = (normed_in * gain_a).astype(jnp.bfloat16)
    both = project(projected, w_in)
    glu_value = both[..., :model_width]
    glu_gate = jax.nn.sigmoid(both[..., model_width:])
    gated = glu_value * glu_gate * padding
    conv_out = depthwise(gated, taps)
    normed_mid, inv_mid = layer_norm(conv_out)
    scaled_mid = normed_mid * gain_b
    swished = (scaled_mid * jax.nn.sigmoid(scaled_mid)).astype(jnp.bfloat16)
    result = (source + project(swished, w_out)).astype(jnp.bfloat16)
    return (
        result,
        (
            normed_in,
            inv_in,
            projected,
            glu_value,
            glu_gate,
            gated,
            normed_mid,
            inv_mid,
            scaled_mid,
            swished,
        ),
    )


def section_backward(upstream, w_in, w_out, gain_a, gain_b, taps, padding, saved):
    (
        normed_in,
        inv_in,
        projected,
        glu_value,
        glu_gate,
        gated,
        normed_mid,
        inv_mid,
        scaled_mid,
        swished,
    ) = saved
    kernel = taps.shape[0]
    half = kernel // 2
    length = upstream.shape[1]
    swish_grad = project_back(upstream, w_out)
    sigmoid_mid = jax.nn.sigmoid(scaled_mid)
    scaled_grad = swish_grad * (sigmoid_mid + scaled_mid * sigmoid_mid * (1.0 - sigmoid_mid))
    gain_b_grad = jnp.sum(scaled_grad * normed_mid, axis=(0, 1))
    conv_grad = norm_grad(scaled_grad * gain_b, normed_mid, inv_mid)
    padded_in = jnp.pad(gated, ((0, 0), (half, half), (0, 0)))
    taps_grad = jnp.stack(
        [
            jnp.sum(conv_grad * padded_in[:, offset : offset + length, :], axis=(0, 1))
            for offset in range(kernel)
        ]
    )
    padded_grad = jnp.pad(conv_grad, ((0, 0), (half, half), (0, 0)))
    gated_grad = padded_grad[:, 2 * half : 2 * half + length, :] * taps[0]
    for offset in range(1, kernel):
        gated_grad = (
            gated_grad
            + padded_grad[:, 2 * half - offset : 2 * half - offset + length, :] * taps[offset]
        )
    gated_grad = gated_grad * padding
    value_grad = gated_grad * glu_gate
    gate_grad = gated_grad * glu_value * glu_gate * (1.0 - glu_gate)
    proj_grad = jnp.concatenate([value_grad, gate_grad], axis=-1).astype(jnp.bfloat16)
    input_side = project_back(proj_grad, w_in)
    gain_a_grad = jnp.sum(input_side * normed_in, axis=(0, 1))
    input_grad = (
        upstream.astype(jnp.float32) + norm_grad(input_side * gain_a, normed_in, inv_in)
    ).astype(jnp.bfloat16)
    return (input_grad, proj_grad, (gain_a_grad, gain_b_grad, taps_grad))


def saved_zeros(micro_count, frames_len, model_width):
    wide = (micro_count, 1, frames_len, model_width)
    narrow = (micro_count, 1, frames_len, 1)
    return (
        jnp.zeros(wide, jnp.float32),
        jnp.zeros(narrow, jnp.float32),
        jnp.zeros(wide, jnp.bfloat16),
        jnp.zeros(wide, jnp.float32),
        jnp.zeros(wide, jnp.float32),
        jnp.zeros(wide, jnp.float32),
        jnp.zeros(wide, jnp.float32),
        jnp.zeros(narrow, jnp.float32),
        jnp.zeros(wide, jnp.float32),
        jnp.zeros(wide, jnp.bfloat16),
    )


def put_slot(buffers, values, micro_slot):
    return jax.tree.map(
        lambda buffer, value: lax.dynamic_update_index_in_dim(buffer, value, micro_slot, 0),
        buffers,
        values,
    )


def take_slot(buffers, micro_slot):
    return jax.tree.map(
        lambda buffer: lax.dynamic_index_in_dim(buffer, micro_slot, 0, keepdims=False), buffers
    )


def local(frames, cotangent, lengths, w_in, w_out, gain_pre, gain_mid, w_depth):
    section_count = lax.axis_size("section")
    section_index = lax.axis_index("section")
    micro_count = frames.shape[0]
    frames_len = frames.shape[2]
    model_width = frames.shape[3]
    moments = micro_count + section_count - 1
    scale = 1.0 / math.sqrt(
        micro_count * frames_len * lax.axis_size("fsdp") * lax.axis_size("batch")
    )
    w_in_full, w_out_full = (
        lax.all_gather(w_in[0], "fsdp", axis=0, tiled=True),
        lax.all_gather(w_out[0], "fsdp", axis=0, tiled=True),
    )
    gain_a = gain_pre[0]
    gain_b = gain_mid[0]
    taps = w_depth[0]
    positions = jnp.arange(frames_len, dtype=jnp.int32)

    def frame_padding(micro_slot):
        return (positions < lengths[micro_slot, 0]).astype(jnp.float32).reshape(1, frames_len, 1)

    stored = saved_zeros(micro_count, frames_len, model_width)
    blank = jnp.zeros((1, frames_len, model_width), jnp.bfloat16)
    outgoing = blank
    for moment in range(moments):
        if moment > 0:
            incoming = from_behind(outgoing, "section", 1)
        else:
            incoming = blank
        if moment < micro_count:
            section_input = jnp.where(section_index == 0, frames[moment], incoming)
        else:
            section_input = incoming
        micro_index = moment - section_index
        active = (micro_index >= 0) & (micro_index < micro_count)
        micro_slot = jnp.clip(micro_index, 0, micro_count - 1)

        def advance(operands, micro_slot=micro_slot):
            current, buffers = operands
            result, saved = section_forward(
                current, w_in_full, w_out_full, gain_a, gain_b, taps, frame_padding(micro_slot)
            )
            return (result, put_slot(buffers, saved, micro_slot))

        def bypass(operands):
            return (jnp.zeros_like(operands[0]), operands[1])

        outgoing, stored = lax.cond(active, advance, bypass, (section_input, stored))
    row_buffers = (
        jnp.zeros((micro_count, frames_len, model_width), jnp.bfloat16),
        jnp.zeros((micro_count, frames_len, 2 * model_width), jnp.bfloat16),
        jnp.zeros((micro_count, frames_len, model_width), jnp.bfloat16),
        jnp.zeros((micro_count, frames_len, model_width), jnp.bfloat16),
        jnp.zeros((micro_count, frames_len, model_width), jnp.bfloat16),
    )
    small_sums = (
        jnp.zeros((model_width,), jnp.float32),
        jnp.zeros((model_width,), jnp.float32),
        jnp.zeros(taps.shape, jnp.float32),
    )
    returning = blank
    for moment in range(moments):
        if moment > 0:
            incoming = from_behind(returning, "section", -1)
        else:
            incoming = blank
        if moment < micro_count:
            upstream = jnp.where(section_index == section_count - 1, cotangent[moment], incoming)
        else:
            upstream = incoming
        micro_index = moment - (section_count - 1 - section_index)
        active = (micro_index >= 0) & (micro_index < micro_count)
        micro_slot = jnp.clip(micro_index, 0, micro_count - 1)

        def retreat(operands, micro_slot=micro_slot):
            current, buffers, totals = operands
            padding = frame_padding(micro_slot)
            saved = take_slot(stored, micro_slot)
            input_grad, proj_grad, minor_grads = section_backward(
                current, w_in_full, w_out_full, gain_a, gain_b, taps, padding, saved
            )
            row_values = (saved[2][0], proj_grad[0], saved[9][0], current[0], input_grad[0])
            buffers = put_slot(buffers, row_values, micro_slot)
            totals = tuple((total + extra for total, extra in zip(totals, minor_grads)))
            return (input_grad, buffers, totals)

        def hold(operands):
            return (jnp.zeros_like(operands[0]), operands[1], operands[2])

        returning, row_buffers, small_sums = lax.cond(
            active, retreat, hold, (upstream, row_buffers, small_sums)
        )
    total_rows = micro_count * frames_len
    proj_rows = row_buffers[0].reshape(total_rows, model_width)
    grad_rows = row_buffers[1].reshape(total_rows, 2 * model_width)
    swish_rows = row_buffers[2].reshape(total_rows, model_width)
    upstream_rows = row_buffers[3].reshape(total_rows, model_width)
    term_in = lax.dot_general(
        proj_rows, grad_rows, (((0,), (0,)), ((), ())), preferred_element_type=jnp.float32
    )
    term_out = lax.dot_general(
        swish_rows, upstream_rows, (((0,), (0,)), ((), ())), preferred_element_type=jnp.float32
    )
    rounded_in = lax.optimization_barrier(term_in.astype(jnp.bfloat16)).astype(jnp.float32)
    rounded_out = lax.optimization_barrier(term_out.astype(jnp.bfloat16)).astype(jnp.float32)
    shares = (
        lax.psum_scatter(
            rounded_in.astype(jnp.bfloat16), "fsdp", scatter_dimension=0, tiled=True
        ).astype(jnp.float32),
        lax.psum_scatter(
            rounded_out.astype(jnp.bfloat16), "fsdp", scatter_dimension=0, tiled=True
        ).astype(jnp.float32),
    )
    grad_in, grad_out = (
        lax.psum(shares[0].astype(jnp.bfloat16), "batch").astype(jnp.float32),
        lax.psum(shares[1].astype(jnp.bfloat16), "batch").astype(jnp.float32),
    )
    small_total = lax.psum((small_sums[0], small_sums[1], small_sums[2]), ("fsdp", "batch"))
    input_grads = row_buffers[4].reshape(1, micro_count, 1, frames_len, model_width)
    return (
        input_grads,
        (scale * grad_in)[None],
        (scale * grad_out)[None],
        (scale * small_total[0])[None],
        (scale * small_total[1])[None],
        (scale * small_total[2])[None],
    )


TILE = 256
LANES = 128
EDGE = 16
IN_PIECES = 8
OUT_PIECES = 4
IN_FLIGHT = 3


def pipeline_kernel(
    dims,
    frames,
    cotangent,
    pad,
    w_in,
    w_out,
    gain_pre,
    gain_mid,
    taps,
    ig,
    total,
    small_total,
    win,
    wout,
    xin,
    xout,
    nin,
    inv_in,
    proj,
    val,
    gate,
    gpad,
    nmid,
    inv_mid,
    sw,
    mid,
    cpad,
    tg,
    lp,
    ls,
    right,
    part,
    arrived,
    conv_grad,
    small,
    small_y,
    small_sum,
    small_a,
    small_b,
    w_ys,
    w_yr,
    w_zs,
    w_zr,
    w_loc,
    turn,
    f_s,
    f_r,
    b_s,
    b_r,
    yp_s,
    yp_r,
    ysw_s,
    ysw_r,
    yu_s,
    yu_r,
    yg_s,
    yg_r,
    sy_s,
    sy_r,
    a_s,
    a_r,
    c_s,
    c_r,
    t_s,
    t_r,
):
    steps, group, length, width, kernel = dims
    rows = group * length
    tiles = width // TILE
    half = width // 2
    f32, bf16 = jnp.float32, jnp.bfloat16
    sections = lax.axis_size("section")
    sec = lax.axis_index("section")
    fs = lax.axis_index("fsdp")
    ba = lax.axis_index("batch")
    other = 1 - fs
    mate = ba + 1 - 2 * lax.rem(ba, 2)
    parity = lax.rem(ba, 2)
    edge = (ba == 0) | (ba == 3)
    inner = jnp.where(ba == 0, 1, 2)
    outer = jnp.where(ba == 1, 0, 3)
    opposite = 3 - ba

    def remote(src, dst, send, recv, **where):
        return pltpu.make_async_remote_copy(
            src_ref=src,
            dst_ref=dst,
            send_sem=send,
            recv_sem=recv,
            device_id=where,
            device_id_type=pl.DeviceIdType.MESH,
        )

    def tile(j, base=0):
        return pl.ds(pl.multiple_of(base + j * TILE, TILE), TILE)

    barrier = pltpu.get_barrier_semaphore()
    for where in (
        {"section": lax.rem(sec + 1, sections)},
        {"section": lax.rem(sec + sections - 1, sections)},
        {"fsdp": other},
        {"batch": lax.rem(ba + 1, 4)},
        {"batch": lax.rem(ba + 3, 4)},
    ):
        pl.semaphore_signal(barrier, inc=1, device_id=where, device_id_type=pl.DeviceIdType.MESH)
    pl.semaphore_wait(barrier, 5)

    pieces = [(w_in, win, half // 16, 2 * i) for i in range(IN_PIECES)]
    pieces += [(w_out, wout, half // 8, 2 * i) for i in range(OUT_PIECES)]

    def span(size, first, which, owner=None):
        begin = (first + which) * size
        if owner is not None:
            begin = owner * half + begin
        return pl.ds(pl.multiple_of(begin, 16), size)

    def over_y(i):
        src, dst, size, first = pieces[i]
        return remote(
            src.at[span(size, first, parity)],
            dst.at[span(size, first, parity, fs)],
            w_ys.at[i],
            w_yr.at[i],
            fsdp=other,
        )

    def over_z(i):
        _, dst, size, first = pieces[i]
        block = dst.at[span(size, first, parity, other)]
        return remote(block, block, w_zs.at[i], w_zr.at[i], batch=mate)

    own = pl.ds(pl.multiple_of(fs * half, 16), half)
    own_in = pltpu.make_async_copy(w_in, win.at[own], w_loc.at[0])
    own_out = pltpu.make_async_copy(w_out, wout.at[own], w_loc.at[1])
    own_in.start()
    own_out.start()

    gpad[...] = jnp.zeros_like(gpad)
    cpad[...] = jnp.zeros_like(cpad)
    tg[...] = jnp.zeros_like(tg)
    small[...] = jnp.zeros_like(small)

    all_pieces = IN_PIECES + OUT_PIECES
    second_of_pair = lax.rem(sec, 2) == 1

    @pl.when(second_of_pair)
    def _():
        pl.semaphore_wait(turn, 1)

    for i in range(IN_FLIGHT):
        over_y(i).start()

    def pass_on(i):
        over_y(i).wait_recv()
        over_z(i).start()
        if i + IN_FLIGHT < all_pieces:
            over_y(i).wait_send()
            over_y(i + IN_FLIGHT).start()

    for i in range(IN_PIECES):
        pass_on(i)
    own_in.wait()
    for i in range(IN_PIECES):
        over_z(i).wait_recv()

    def rest_of_weights():
        for i in range(IN_PIECES, all_pieces):
            pass_on(i)

        @pl.when(jnp.logical_not(second_of_pair))
        def _():
            pl.semaphore_signal(
                turn,
                inc=1,
                device_id={"section": sec + 1},
                device_id_type=pl.DeviceIdType.MESH,
            )

        own_out.wait()
        for i in range(IN_PIECES, all_pieces):
            over_z(i).wait_recv()

    @pl.when(sec > 0)
    def _():
        rest_of_weights()

    mine = pl.ds(pl.multiple_of(fs * half, LANES), half)
    theirs = pl.ds(pl.multiple_of(other * half, LANES), half)

    def send_forward(s):
        return remote(xout.at[s], xin.at[s], f_s.at[s], f_r.at[s], section=lax.rem(sec + 1, sections))

    def send_backward(s):
        return remote(
            ig.at[s],
            right.at[s, :, pl.ds(2 * width, width)],
            b_s.at[s],
            b_r.at[s],
            section=lax.rem(sec + sections - 1, sections),
        )

    def send_proj(s):
        return remote(proj.at[s, :, theirs], lp.at[steps + s], yp_s.at[s], yp_r.at[s], fsdp=other)

    def send_sw(s):
        return remote(sw.at[s, :, theirs], ls.at[steps + s], ysw_s.at[s], ysw_r.at[s], fsdp=other)

    def send_up(s):
        cols = pl.ds(2 * width, width)
        return remote(
            right.at[s, :, cols], right.at[steps + s, :, cols], yu_s.at[s], yu_r.at[s], fsdp=other
        )

    def send_grad(s):
        cols = pl.ds(0, 2 * width)
        return remote(
            right.at[s, :, cols], right.at[steps + s, :, cols], yg_s.at[s], yg_r.at[s], fsdp=other
        )

    def norm_stats(values):
        mean_value = jnp.sum(values, axis=-1, keepdims=True) * (1.0 / width)
        centred = values - mean_value
        inv = lax.rsqrt(jnp.sum(centred * centred, axis=-1, keepdims=True) * (1.0 / width) + epsilon)
        return centred * inv, inv

    def forward(s, carry):
        @pl.when(sec == 0)
        def _():
            xin[s] = frames[s]

        @pl.when(sec > 0)
        def _():
            send_forward(s).wait_recv()

        normed, inv = norm_stats(xin[s].astype(f32))
        nin[s] = normed
        inv_in[s] = inv
        proj[s] = (normed * gain_pre[...]).astype(bf16)
        send_proj(s).start()
        lp[s] = proj[s, :, mine]

        def first(j, carry):
            left = proj[s]
            v = jnp.dot(left, win[:, tile(j)], preferred_element_type=f32)
            g = jax.nn.sigmoid(
                jnp.dot(left, win[:, tile(j, width)], preferred_element_type=f32)
            )
            val[s, :, tile(j)] = v
            gate[s, :, tile(j)] = g
            gated = v * g * pad[s]
            for m in range(group):
                gpad[s * group + m, EDGE : EDGE + length, tile(j)] = gated[
                    m * length : (m + 1) * length
                ]
            for m in range(group):
                for c in range(TILE // LANES):
                    cols = pl.ds(pl.multiple_of(j * TILE + c * LANES, LANES), LANES)
                    acc = jnp.zeros((length, LANES), f32)
                    for b in range(8):
                        rolled = gpad[s * group + m, b : b + length + 24, cols]
                        for a in range(4):
                            k = 8 * a + b - 1
                            if 0 <= k < kernel:
                                acc = acc + rolled[8 * a : 8 * a + length] * taps[k : k + 1, cols]
                    mid[m * length : (m + 1) * length, cols] = acc
            return carry

        lax.fori_loop(0, tiles, first, 0)
        normed2, inv2 = norm_stats(mid[...])
        nmid[s] = normed2
        inv_mid[s] = inv2
        scaled = normed2 * gain_mid[...]
        sw[s] = (scaled * jax.nn.sigmoid(scaled)).astype(bf16)
        send_sw(s).start()
        ls[s] = sw[s, :, mine]

        @pl.when((sec == 0) & (s == 0))
        def _():
            rest_of_weights()

        @pl.when(sec < sections - 1)
        def _():
            def second(j, carry):
                out = jnp.dot(sw[s], wout[:, tile(j)], preferred_element_type=f32)
                xout[s, :, tile(j)] = (xin[s, :, tile(j)].astype(f32) + out).astype(bf16)
                return carry

            lax.fori_loop(0, tiles, second, 0)
            send_forward(s).start()

        return carry

    lax.fori_loop(0, steps, forward, 0)

    nt = (((1,), (1,)), ((), ()))

    def backward(s, carry):
        @pl.when(sec == sections - 1)
        def _():
            right[s, :, pl.ds(2 * width, width)] = cotangent[s]

        @pl.when(sec < sections - 1)
        def _():
            send_backward(s).wait_recv()

        send_up(s).start()
        zero = jnp.zeros((rows, 1), f32)

        def first(j, sums):
            up = right[s, :, pl.ds(2 * width, width)]
            sg = lax.dot_general(up, wout[tile(j), :], nt, preferred_element_type=f32)
            nm = nmid[s, :, tile(j)]
            gb = gain_mid[:, tile(j)]
            scaled = nm * gb
            sig = jax.nn.sigmoid(scaled)
            scg = sg * (sig + scaled * sig * (1.0 - sig))
            small[1:2, tile(j)] += jnp.sum(scg * nm, axis=0, keepdims=True)
            z = scg * gb
            mid[:, tile(j)] = z
            return (
                sums[0] + jnp.sum(z, axis=-1, keepdims=True),
                sums[1] + jnp.sum(z * nm, axis=-1, keepdims=True),
            )

        s1, s2 = lax.fori_loop(0, tiles, first, (zero, zero))
        s1 = s1 * (1.0 / width)
        s2 = s2 * (1.0 / width)

        def second(j, carry):
            cols = pl.ds(pl.multiple_of(j * LANES, LANES), LANES)
            gate_cols = pl.ds(pl.multiple_of(width + j * LANES, LANES), LANES)
            cg_all = (mid[:, cols] - s1 - nmid[s, :, cols] * s2) * inv_mid[s]
            conv_grad[:, cols] = cg_all
            for m in range(group):
                span_m = slice(m * length, (m + 1) * length)
                cg = cg_all[span_m]
                cpad[m, EDGE : EDGE + length, :] = cg
                acc = jnp.zeros((length, LANES), f32)
                for b in range(8):
                    rolled = cpad[m, b : b + length + 24, :]
                    for a in range(4):
                        k = kernel - 1 - (8 * a + b - 1)
                        if 0 <= k < kernel:
                            acc = acc + rolled[8 * a : 8 * a + length] * taps[k : k + 1, cols]
                acc = acc * pad[s, span_m]
                g = gate[s, span_m, cols]
                vg = acc * g
                right[s, span_m, cols] = vg.astype(bf16)
                right[s, span_m, gate_cols] = (
                    acc * val[s, span_m, cols] * g * (1.0 - g)
                ).astype(bf16)
            return carry

        lax.fori_loop(0, width // LANES, second, 0)
        send_grad(s).start()

        def third(j, sums):
            pg = right[s, :, pl.ds(0, 2 * width)]
            ins = lax.dot_general(pg, win[tile(j), :], nt, preferred_element_type=f32)
            nv = nin[s, :, tile(j)]
            small[0:1, tile(j)] += jnp.sum(ins * nv, axis=0, keepdims=True)
            z = ins * gain_pre[:, tile(j)]
            mid[:, tile(j)] = z
            return (
                sums[0] + jnp.sum(z, axis=-1, keepdims=True),
                sums[1] + jnp.sum(z * nv, axis=-1, keepdims=True),
            )

        m1, m2 = lax.fori_loop(0, tiles, third, (zero, zero))
        m1 = m1 * (1.0 / width)
        m2 = m2 * (1.0 / width)
        up = right[s, :, pl.ds(2 * width, width)].astype(f32)
        ig[s] = (up + (mid[...] - m1 - nin[s] * m2) * inv_in[s]).astype(bf16)

        @pl.when(sec > 0)
        def _():
            send_backward(s).start()

        def fourth(j, carry):
            cols = pl.ds(pl.multiple_of(j * LANES, LANES), LANES)
            for m in range(group):
                cg = conv_grad[m * length : (m + 1) * length, cols]
                for b in range(8):
                    rolled = gpad[s * group + m, b : b + length + 24, cols]
                    for a in range(4):
                        k = 8 * a + b - 1
                        if 0 <= k < kernel:
                            term = cg * rolled[8 * a : 8 * a + length]
                            tg[k, :, cols] += jnp.sum(term.reshape(length // 8, 8, LANES), axis=0)
            return carry

        lax.fori_loop(0, width // LANES, fourth, 0)
        return carry

    lax.fori_loop(0, steps, backward, 0)

    small[8 : 8 + kernel] = jnp.sum(tg[...], axis=1)
    swap = remote(small, small_y, sy_s, sy_r, fsdp=other)
    swap.start()

    parts = 6 * tiles
    depth = half // 2

    def place(p):
        at = lax.rem(p // 2 + 2 * tiles, 3 * tiles)
        return pl.ds(pl.multiple_of(lax.rem(p, 2) * depth, 16), depth), tile(at)

    def to_inner(p):
        where = place(p)
        return remote(part.at[where], arrived.at[where], a_s.at[p], a_r.at[p], batch=inner)

    def across(p):
        where = place(p)
        return remote(part.at[where], total.at[where], c_s.at[p], c_r.at[p], batch=opposite)

    def to_outer(p):
        where = place(p)
        return remote(total.at[where], total.at[where], t_s.at[p], t_r.at[p], batch=outer)

    small_to_inner = remote(small_sum, small_a, a_s.at[parts], a_r.at[parts], batch=inner)
    small_across = remote(small_sum, small_b, c_s.at[parts], c_r.at[parts], batch=opposite)
    small_to_outer = remote(small_total, small_total, t_s.at[parts], t_r.at[parts], batch=outer)

    tn = (((0,), (0,)), ((), ()))

    def finish(p):
        where = place(p)
        across(p).wait_recv()
        across(p).wait_send()
        total[where] = (part[where].astype(f32) + total[where].astype(f32)).astype(bf16)
        to_outer(p).start()

    def terms(left_ref, first_tile, count):
        def one(order, carry):
            cols = tile(lax.rem(order + 2 * tiles, 3 * tiles))
            left = left_ref[...].reshape(2 * steps * rows, half)
            block = right[:, :, cols].reshape(2 * steps * rows, TILE)
            part[:, cols] = lax.dot_general(
                left, block, tn, preferred_element_type=f32
            ).astype(bf16)

            @pl.when(edge)
            def _():
                def send(p, carry):
                    @pl.when(p >= IN_FLIGHT)
                    def _():
                        to_inner(p - IN_FLIGHT).wait_send()

                    to_inner(p).start()
                    return carry

                lax.fori_loop(2 * order, 2 * order + 2, send, 0)

            @pl.when(jnp.logical_not(edge))
            def _():
                def meet(p, carry):
                    where = place(p)
                    to_inner(p).wait_recv()
                    part[where] = (
                        part[where].astype(f32) + arrived[where].astype(f32)
                    ).astype(bf16)
                    across(p).start()

                    @pl.when(p > 0)
                    def _():
                        finish(p - 1)

                    return carry

                lax.fori_loop(2 * order, 2 * order + 2, meet, 0)

            return carry

        lax.fori_loop(first_tile, first_tile + count, one, 0)

    def arrivals_out(s, carry):
        send_sw(s).wait_recv()
        send_up(s).wait_recv()
        return carry

    def arrivals_in(s, carry):
        send_proj(s).wait_recv()
        send_grad(s).wait_recv()
        return carry

    lax.fori_loop(0, steps, arrivals_out, 0)
    terms(ls, 0, tiles)
    lax.fori_loop(0, steps, arrivals_in, 0)
    swap.wait_recv()
    small_sum[...] = small[...] + small_y[...]

    @pl.when(edge)
    def _():
        small_to_inner.start()

    @pl.when(jnp.logical_not(edge))
    def _():
        small_to_inner.wait_recv()
        small_sum[...] = small_sum[...] + small_a[...]
        small_across.start()

    terms(lp, tiles, 2 * tiles)

    @pl.when(jnp.logical_not(edge))
    def _():
        small_across.wait_recv()
        small_across.wait_send()
        small_total[...] = small_sum[...] + small_b[...]
        small_to_outer.start()
        finish(parts - 1)

        def sent(p, carry):
            to_outer(p).wait_send()
            return carry

        lax.fori_loop(0, parts, sent, 0)
        small_to_outer.wait_send()

    @pl.when(edge)
    def _():
        def left_over(p, carry):
            to_inner(p).wait_send()
            return carry

        def done(p, carry):
            to_outer(p).wait_recv()
            return carry

        lax.fori_loop(parts - IN_FLIGHT, parts, left_over, 0)
        lax.fori_loop(0, parts, done, 0)
        small_to_inner.wait_send()
        small_to_outer.wait_recv()

    for i in range(all_pieces):
        if i + IN_FLIGHT >= all_pieces:
            over_y(i).wait_send()
        over_z(i).wait_send()
    swap.wait_send()

    def drained(s, carry):
        send_proj(s).wait_send()
        send_sw(s).wait_send()
        send_up(s).wait_send()
        send_grad(s).wait_send()

        @pl.when(sec < sections - 1)
        def _():
            send_forward(s).wait_send()

        @pl.when(sec > 0)
        def _():
            send_backward(s).wait_send()

        return carry

    lax.fori_loop(0, steps, drained, 0)


def fused(frames, cotangent, lengths, w_in, w_out, gain_pre, gain_mid, w_depth):
    micro_count, _, length, width = frames.shape
    kernel = w_depth.shape[1]
    group = GROUP
    steps = micro_count // group
    rows = group * length
    half = w_in.shape[1]
    scale = 1.0 / math.sqrt(micro_count * length * lax.axis_size("fsdp") * lax.axis_size("batch"))
    positions = jnp.arange(length, dtype=jnp.int32)
    pad = (positions[None, :] < lengths).astype(jnp.float32).reshape(steps, rows, 1)
    f32, bf16 = jnp.float32, jnp.bfloat16
    parts = 6 * (width // TILE)
    small_rows = 8 + -(-kernel // 8) * 8
    vmem = pl.BlockSpec(memory_space=pltpu.VMEM)
    hbm = pl.BlockSpec(memory_space=pl.ANY)

    def buf(*shape, dtype=f32):
        return pltpu.VMEM(shape, dtype)

    def sem(*shape):
        return pltpu.SemaphoreType.DMA(shape)

    ig, total, small = pl.pallas_call(
        functools.partial(pipeline_kernel, (steps, group, length, width, kernel)),
        out_shape=(
            jax.ShapeDtypeStruct((steps, rows, width), bf16),
            jax.ShapeDtypeStruct((half, 3 * width), bf16),
            jax.ShapeDtypeStruct((small_rows, width), f32),
        ),
        in_specs=[vmem, vmem, vmem, hbm, hbm, vmem, vmem, vmem],
        out_specs=(vmem, vmem, vmem),
        scratch_shapes=[
            buf(width, 2 * width, dtype=bf16),
            buf(width, width, dtype=bf16),
            buf(steps, rows, width, dtype=bf16),
            buf(steps, rows, width, dtype=bf16),
            buf(steps, rows, width),
            buf(steps, rows, 1),
            buf(steps, rows, width, dtype=bf16),
            buf(steps, rows, width),
            buf(steps, rows, width),
            buf(micro_count, length + 2 * EDGE, width),
            buf(steps, rows, width),
            buf(steps, rows, 1),
            buf(steps, rows, width, dtype=bf16),
            buf(rows, width),
            buf(group, length + 2 * EDGE, LANES),
            buf(kernel, 8, width),
            buf(2 * steps, rows, half, dtype=bf16),
            buf(2 * steps, rows, half, dtype=bf16),
            buf(2 * steps, rows, 3 * width, dtype=bf16),
            buf(half, 3 * width, dtype=bf16),
            buf(half, 3 * width, dtype=bf16),
            buf(rows, width),
            buf(small_rows, width),
            buf(small_rows, width),
            buf(small_rows, width),
            buf(small_rows, width),
            buf(small_rows, width),
            *[sem(IN_PIECES + OUT_PIECES) for _ in range(4)],
            sem(2),
            pltpu.SemaphoreType.REGULAR,
            *[sem(steps) for _ in range(12)],
            pltpu.SemaphoreType.DMA,
            pltpu.SemaphoreType.DMA,
            *[sem(parts + 1) for _ in range(6)],
        ],
        compiler_params=pltpu.CompilerParams(
            collective_id=0, has_side_effects=True, vmem_limit_bytes=62 * 1024 * 1024
        ),
    )(
        frames.reshape(steps, rows, width),
        cotangent.reshape(steps, rows, width),
        pad,
        w_in[0],
        w_out[0],
        gain_pre,
        gain_mid,
        w_depth[0],
    )
    return (
        ig.reshape(1, micro_count, 1, length, width),
        (scale * total[:, : 2 * width].astype(f32))[None],
        (scale * total[:, 2 * width :].astype(f32))[None],
        (scale * small[0])[None],
        (scale * small[1])[None],
        (scale * small[8 : 8 + kernel])[None],
    )


def solution(mesh):
    in_specs = (
        P(None, ("fsdp", "batch"), None, None),
        P(None, ("fsdp", "batch"), None, None),
        P(None, ("fsdp", "batch")),
        P("section", "fsdp", None),
        P("section", "fsdp", None),
        P("section", None),
        P("section", None),
        P("section", None, None),
    )
    out_specs = (
        P("section", None, ("fsdp", "batch"), None, None),
        P("section", "fsdp", None),
        P("section", "fsdp", None),
        P("section", None),
        P("section", None),
        P("section", None, None),
    )
    paired = mesh.shape["fsdp"] == 2 and mesh.shape["batch"] == 4
    body = fused if paired else local
    return jax.shard_map(body, mesh=mesh, in_specs=in_specs, out_specs=out_specs, check_vma=False)
```

```python
import functools
import math

import jax
import jax.numpy as jnp
from jax import lax
from jax.experimental import pallas as pl
from jax.experimental.pallas import tpu as pltpu
from jax.sharding import PartitionSpec as P

epsilon = 1e-05
GROUP = 1


def from_behind(x, axis, by):
    peers = lax.axis_size(axis)
    pairs = [(i, i + by) for i in range(peers) if 0 <= i + by < peers]
    return lax.ppermute(x, axis, pairs)


def layer_norm(values):
    mean_value = jnp.mean(values, axis=-1, keepdims=True)
    centred = values - mean_value
    inv_scale = lax.rsqrt(jnp.mean(centred * centred, axis=-1, keepdims=True) + epsilon)
    return (centred * inv_scale, inv_scale)


def norm_grad(upstream, normed, inv_scale):
    return (
        upstream
        - jnp.mean(upstream, axis=-1, keepdims=True)
        - normed * jnp.mean(upstream * normed, axis=-1, keepdims=True)
    ) * inv_scale


def project(left, right):
    batch_rows, length, inner = left.shape
    flat = jnp.dot(
        left.reshape(batch_rows * length, inner), right, preferred_element_type=jnp.float32
    )
    return flat.reshape(batch_rows, length, right.shape[1])


def project_back(left, right):
    batch_rows, length, inner = left.shape
    flat = lax.dot_general(
        left.reshape(batch_rows * length, inner),
        right,
        (((1,), (1,)), ((), ())),
        preferred_element_type=jnp.float32,
    )
    return flat.reshape(batch_rows, length, right.shape[0])


def depthwise(values, taps):
    kernel = taps.shape[0]
    half = kernel // 2
    length = values.shape[1]
    padded = jnp.pad(values, ((0, 0), (half, half), (0, 0)))
    total = padded[:, 0:length, :] * taps[0]
    for offset in range(1, kernel):
        total = total + padded[:, offset : offset + length, :] * taps[offset]
    return total


def section_forward(frames, w_in, w_out, gain_a, gain_b, taps, padding):
    model_width = frames.shape[-1]
    source = frames.astype(jnp.float32)
    normed_in, inv_in = layer_norm(source)
    projected = (normed_in * gain_a).astype(jnp.bfloat16)
    both = project(projected, w_in)
    glu_value = both[..., :model_width]
    glu_gate = jax.nn.sigmoid(both[..., model_width:])
    gated = glu_value * glu_gate * padding
    conv_out = depthwise(gated, taps)
    normed_mid, inv_mid = layer_norm(conv_out)
    scaled_mid = normed_mid * gain_b
    swished = (scaled_mid * jax.nn.sigmoid(scaled_mid)).astype(jnp.bfloat16)
    result = (source + project(swished, w_out)).astype(jnp.bfloat16)
    return (
        result,
        (
            normed_in,
            inv_in,
            projected,
            glu_value,
            glu_gate,
            gated,
            normed_mid,
            inv_mid,
            scaled_mid,
            swished,
        ),
    )


def section_backward(upstream, w_in, w_out, gain_a, gain_b, taps, padding, saved):
    (
        normed_in,
        inv_in,
        projected,
        glu_value,
        glu_gate,
        gated,
        normed_mid,
        inv_mid,
        scaled_mid,
        swished,
    ) = saved
    kernel = taps.shape[0]
    half = kernel // 2
    length = upstream.shape[1]
    swish_grad = project_back(upstream, w_out)
    sigmoid_mid = jax.nn.sigmoid(scaled_mid)
    scaled_grad = swish_grad * (sigmoid_mid + scaled_mid * sigmoid_mid * (1.0 - sigmoid_mid))
    gain_b_grad = jnp.sum(scaled_grad * normed_mid, axis=(0, 1))
    conv_grad = norm_grad(scaled_grad * gain_b, normed_mid, inv_mid)
    padded_in = jnp.pad(gated, ((0, 0), (half, half), (0, 0)))
    taps_grad = jnp.stack(
        [
            jnp.sum(conv_grad * padded_in[:, offset : offset + length, :], axis=(0, 1))
            for offset in range(kernel)
        ]
    )
    padded_grad = jnp.pad(conv_grad, ((0, 0), (half, half), (0, 0)))
    gated_grad = padded_grad[:, 2 * half : 2 * half + length, :] * taps[0]
    for offset in range(1, kernel):
        gated_grad = (
            gated_grad
            + padded_grad[:, 2 * half - offset : 2 * half - offset + length, :] * taps[offset]
        )
    gated_grad = gated_grad * padding
    value_grad = gated_grad * glu_gate
    gate_grad = gated_grad * glu_value * glu_gate * (1.0 - glu_gate)
    proj_grad = jnp.concatenate([value_grad, gate_grad], axis=-1).astype(jnp.bfloat16)
    input_side = project_back(proj_grad, w_in)
    gain_a_grad = jnp.sum(input_side * normed_in, axis=(0, 1))
    input_grad = (
        upstream.astype(jnp.float32) + norm_grad(input_side * gain_a, normed_in, inv_in)
    ).astype(jnp.bfloat16)
    return (input_grad, proj_grad, (gain_a_grad, gain_b_grad, taps_grad))


def saved_zeros(micro_count, frames_len, model_width):
    wide = (micro_count, 1, frames_len, model_width)
    narrow = (micro_count, 1, frames_len, 1)
    return (
        jnp.zeros(wide, jnp.float32),
        jnp.zeros(narrow, jnp.float32),
        jnp.zeros(wide, jnp.bfloat16),
        jnp.zeros(wide, jnp.float32),
        jnp.zeros(wide, jnp.float32),
        jnp.zeros(wide, jnp.float32),
        jnp.zeros(wide, jnp.float32),
        jnp.zeros(narrow, jnp.float32),
        jnp.zeros(wide, jnp.float32),
        jnp.zeros(wide, jnp.bfloat16),
    )


def put_slot(buffers, values, micro_slot):
    return jax.tree.map(
        lambda buffer, value: lax.dynamic_update_index_in_dim(buffer, value, micro_slot, 0),
        buffers,
        values,
    )


def take_slot(buffers, micro_slot):
    return jax.tree.map(
        lambda buffer: lax.dynamic_index_in_dim(buffer, micro_slot, 0, keepdims=False), buffers
    )


def local(frames, cotangent, lengths, w_in, w_out, gain_pre, gain_mid, w_depth):
    section_count = lax.axis_size("section")
    section_index = lax.axis_index("section")
    micro_count = frames.shape[0]
    frames_len = frames.shape[2]
    model_width = frames.shape[3]
    moments = micro_count + section_count - 1
    scale = 1.0 / math.sqrt(
        micro_count * frames_len * lax.axis_size("fsdp") * lax.axis_size("batch")
    )
    w_in_full, w_out_full = (
        lax.all_gather(w_in[0], "fsdp", axis=0, tiled=True),
        lax.all_gather(w_out[0], "fsdp", axis=0, tiled=True),
    )
    gain_a = gain_pre[0]
    gain_b = gain_mid[0]
    taps = w_depth[0]
    positions = jnp.arange(frames_len, dtype=jnp.int32)

    def frame_padding(micro_slot):
        return (positions < lengths[micro_slot, 0]).astype(jnp.float32).reshape(1, frames_len, 1)

    stored = saved_zeros(micro_count, frames_len, model_width)
    blank = jnp.zeros((1, frames_len, model_width), jnp.bfloat16)
    outgoing = blank
    for moment in range(moments):
        if moment > 0:
            incoming = from_behind(outgoing, "section", 1)
        else:
            incoming = blank
        if moment < micro_count:
            section_input = jnp.where(section_index == 0, frames[moment], incoming)
        else:
            section_input = incoming
        micro_index = moment - section_index
        active = (micro_index >= 0) & (micro_index < micro_count)
        micro_slot = jnp.clip(micro_index, 0, micro_count - 1)

        def advance(operands, micro_slot=micro_slot):
            current, buffers = operands
            result, saved = section_forward(
                current, w_in_full, w_out_full, gain_a, gain_b, taps, frame_padding(micro_slot)
            )
            return (result, put_slot(buffers, saved, micro_slot))

        def bypass(operands):
            return (jnp.zeros_like(operands[0]), operands[1])

        outgoing, stored = lax.cond(active, advance, bypass, (section_input, stored))
    row_buffers = (
        jnp.zeros((micro_count, frames_len, model_width), jnp.bfloat16),
        jnp.zeros((micro_count, frames_len, 2 * model_width), jnp.bfloat16),
        jnp.zeros((micro_count, frames_len, model_width), jnp.bfloat16),
        jnp.zeros((micro_count, frames_len, model_width), jnp.bfloat16),
        jnp.zeros((micro_count, frames_len, model_width), jnp.bfloat16),
    )
    small_sums = (
        jnp.zeros((model_width,), jnp.float32),
        jnp.zeros((model_width,), jnp.float32),
        jnp.zeros(taps.shape, jnp.float32),
    )
    returning = blank
    for moment in range(moments):
        if moment > 0:
            incoming = from_behind(returning, "section", -1)
        else:
            incoming = blank
        if moment < micro_count:
            upstream = jnp.where(section_index == section_count - 1, cotangent[moment], incoming)
        else:
            upstream = incoming
        micro_index = moment - (section_count - 1 - section_index)
        active = (micro_index >= 0) & (micro_index < micro_count)
        micro_slot = jnp.clip(micro_index, 0, micro_count - 1)

        def retreat(operands, micro_slot=micro_slot):
            current, buffers, totals = operands
            padding = frame_padding(micro_slot)
            saved = take_slot(stored, micro_slot)
            input_grad, proj_grad, minor_grads = section_backward(
                current, w_in_full, w_out_full, gain_a, gain_b, taps, padding, saved
            )
            row_values = (saved[2][0], proj_grad[0], saved[9][0], current[0], input_grad[0])
            buffers = put_slot(buffers, row_values, micro_slot)
            totals = tuple((total + extra for total, extra in zip(totals, minor_grads)))
            return (input_grad, buffers, totals)

        def hold(operands):
            return (jnp.zeros_like(operands[0]), operands[1], operands[2])

        returning, row_buffers, small_sums = lax.cond(
            active, retreat, hold, (upstream, row_buffers, small_sums)
        )
    total_rows = micro_count * frames_len
    proj_rows = row_buffers[0].reshape(total_rows, model_width)
    grad_rows = row_buffers[1].reshape(total_rows, 2 * model_width)
    swish_rows = row_buffers[2].reshape(total_rows, model_width)
    upstream_rows = row_buffers[3].reshape(total_rows, model_width)
    term_in = lax.dot_general(
        proj_rows, grad_rows, (((0,), (0,)), ((), ())), preferred_element_type=jnp.float32
    )
    term_out = lax.dot_general(
        swish_rows, upstream_rows, (((0,), (0,)), ((), ())), preferred_element_type=jnp.float32
    )
    rounded_in = lax.optimization_barrier(term_in.astype(jnp.bfloat16)).astype(jnp.float32)
    rounded_out = lax.optimization_barrier(term_out.astype(jnp.bfloat16)).astype(jnp.float32)
    shares = (
        lax.psum_scatter(
            rounded_in.astype(jnp.bfloat16), "fsdp", scatter_dimension=0, tiled=True
        ).astype(jnp.float32),
        lax.psum_scatter(
            rounded_out.astype(jnp.bfloat16), "fsdp", scatter_dimension=0, tiled=True
        ).astype(jnp.float32),
    )
    grad_in, grad_out = (
        lax.psum(shares[0].astype(jnp.bfloat16), "batch").astype(jnp.float32),
        lax.psum(shares[1].astype(jnp.bfloat16), "batch").astype(jnp.float32),
    )
    small_total = lax.psum((small_sums[0], small_sums[1], small_sums[2]), ("fsdp", "batch"))
    input_grads = row_buffers[4].reshape(1, micro_count, 1, frames_len, model_width)
    return (
        input_grads,
        (scale * grad_in)[None],
        (scale * grad_out)[None],
        (scale * small_total[0])[None],
        (scale * small_total[1])[None],
        (scale * small_total[2])[None],
    )


TILE = 256
LANES = 128
EDGE = 16
IN_PIECES = 8
OUT_PIECES = 4
IN_FLIGHT = 3


def pipeline_kernel(
    dims,
    frames,
    cotangent,
    lengths,
    w_in,
    w_out,
    gain_pre,
    gain_mid,
    taps,
    ig,
    total,
    small_total,
    win,
    wout,
    xin,
    xout,
    nin,
    inv_in,
    proj,
    val,
    gate,
    gpad,
    nmid,
    inv_mid,
    sw,
    mid,
    cpad,
    tg,
    lp,
    ls,
    right,
    part,
    arrived,
    conv_grad,
    pad,
    small,
    small_y,
    small_sum,
    small_a,
    small_b,
    w_ys,
    w_yr,
    w_zs,
    w_zr,
    w_loc,
    turn,
    f_s,
    f_r,
    b_s,
    b_r,
    yp_s,
    yp_r,
    ysw_s,
    ysw_r,
    yu_s,
    yu_r,
    yg_s,
    yg_r,
    sy_s,
    sy_r,
    a_s,
    a_r,
    c_s,
    c_r,
    t_s,
    t_r,
):
    steps, group, length, width, kernel = dims
    rows = group * length
    tiles = width // TILE
    half = width // 2
    f32, bf16 = jnp.float32, jnp.bfloat16
    sections = lax.axis_size("section")
    sec = lax.axis_index("section")
    fs = lax.axis_index("fsdp")
    ba = lax.axis_index("batch")
    other = 1 - fs
    mate = ba + 1 - 2 * lax.rem(ba, 2)
    parity = lax.rem(ba, 2)
    edge = (ba == 0) | (ba == 3)
    inner = jnp.where(ba == 0, 1, 2)
    outer = jnp.where(ba == 1, 0, 3)
    opposite = 3 - ba

    def remote(src, dst, send, recv, **where):
        return pltpu.make_async_remote_copy(
            src_ref=src,
            dst_ref=dst,
            send_sem=send,
            recv_sem=recv,
            device_id=where,
            device_id_type=pl.DeviceIdType.MESH,
        )

    def tile(j, base=0):
        return pl.ds(pl.multiple_of(base + j * TILE, TILE), TILE)

    barrier = pltpu.get_barrier_semaphore()
    for where in (
        {"section": lax.rem(sec + 1, sections)},
        {"section": lax.rem(sec + sections - 1, sections)},
        {"fsdp": other},
        {"batch": lax.rem(ba + 1, 4)},
        {"batch": lax.rem(ba + 3, 4)},
    ):
        pl.semaphore_signal(barrier, inc=1, device_id=where, device_id_type=pl.DeviceIdType.MESH)
    pl.semaphore_wait(barrier, 5)

    pieces = [(w_in, win, half // 16, 2 * i) for i in range(IN_PIECES)]
    pieces += [(w_out, wout, half // 8, 2 * i) for i in range(OUT_PIECES)]

    def span(size, first, which, owner=None):
        begin = (first + which) * size
        if owner is not None:
            begin = owner * half + begin
        return pl.ds(pl.multiple_of(begin, 16), size)

    def over_y(i):
        src, dst, size, first = pieces[i]
        return remote(
            src.at[span(size, first, parity)],
            dst.at[span(size, first, parity, fs)],
            w_ys.at[i],
            w_yr.at[i],
            fsdp=other,
        )

    def over_z(i):
        _, dst, size, first = pieces[i]
        block = dst.at[span(size, first, parity, other)]
        return remote(block, block, w_zs.at[i], w_zr.at[i], batch=mate)

    own = pl.ds(pl.multiple_of(fs * half, 16), half)
    own_in = pltpu.make_async_copy(w_in, win.at[own], w_loc.at[0])
    own_out = pltpu.make_async_copy(w_out, wout.at[own], w_loc.at[1])
    own_in.start()
    own_out.start()

    gpad[...] = jnp.zeros_like(gpad)
    cpad[...] = jnp.zeros_like(cpad)
    tg[...] = jnp.zeros_like(tg)
    small[...] = jnp.zeros_like(small)
    frame = lax.broadcasted_iota(jnp.int32, (length, 1), 0)
    for m in range(steps * group):
        first_row = (m % group) * length
        pad[m // group, first_row : first_row + length] = jnp.where(
            frame < lengths[m, 0], 1.0, 0.0
        ).astype(f32)

    all_pieces = IN_PIECES + OUT_PIECES
    second_of_pair = lax.rem(sec, 2) == 1

    @pl.when(second_of_pair)
    def _():
        pl.semaphore_wait(turn, 1)

    for i in range(IN_FLIGHT):
        over_y(i).start()

    def pass_on(i):
        over_y(i).wait_recv()
        over_z(i).start()
        if i + IN_FLIGHT < all_pieces:
            over_y(i).wait_send()
            over_y(i + IN_FLIGHT).start()

    for i in range(IN_PIECES):
        pass_on(i)
    own_in.wait()
    for i in range(IN_PIECES):
        over_z(i).wait_recv()

    def rest_of_weights():
        for i in range(IN_PIECES, all_pieces):
            pass_on(i)

        @pl.when(jnp.logical_not(second_of_pair))
        def _():
            pl.semaphore_signal(
                turn,
                inc=1,
                device_id={"section": sec + 1},
                device_id_type=pl.DeviceIdType.MESH,
            )

        own_out.wait()
        for i in range(IN_PIECES, all_pieces):
            over_z(i).wait_recv()

    @pl.when(sec > 1)
    def _():
        rest_of_weights()

    mine = pl.ds(pl.multiple_of(fs * half, LANES), half)
    theirs = pl.ds(pl.multiple_of(other * half, LANES), half)

    def send_forward(s):
        return remote(xout.at[s], xin.at[s], f_s.at[s], f_r.at[s], section=lax.rem(sec + 1, sections))

    def send_backward(s):
        return remote(
            ig.at[s],
            right.at[s, :, pl.ds(2 * width, width)],
            b_s.at[s],
            b_r.at[s],
            section=lax.rem(sec + sections - 1, sections),
        )

    def send_proj(s):
        return remote(proj.at[s, :, theirs], lp.at[steps + s], yp_s.at[s], yp_r.at[s], fsdp=other)

    def send_sw(s):
        return remote(sw.at[s, :, theirs], ls.at[steps + s], ysw_s.at[s], ysw_r.at[s], fsdp=other)

    def send_up(s):
        cols = pl.ds(2 * width, width)
        return remote(
            right.at[s, :, cols], right.at[steps + s, :, cols], yu_s.at[s], yu_r.at[s], fsdp=other
        )

    def send_grad(s):
        cols = pl.ds(0, 2 * width)
        return remote(
            right.at[s, :, cols], right.at[steps + s, :, cols], yg_s.at[s], yg_r.at[s], fsdp=other
        )

    def norm_stats(values):
        mean_value = jnp.sum(values, axis=-1, keepdims=True) * (1.0 / width)
        centred = values - mean_value
        inv = lax.rsqrt(jnp.sum(centred * centred, axis=-1, keepdims=True) * (1.0 / width) + epsilon)
        return centred * inv, inv

    def forward(s, carry):
        @pl.when(sec == 0)
        def _():
            xin[s] = frames[s]

        @pl.when(sec > 0)
        def _():
            send_forward(s).wait_recv()

        normed, inv = norm_stats(xin[s].astype(f32))
        nin[s] = normed
        inv_in[s] = inv
        proj[s] = (normed * gain_pre[...]).astype(bf16)
        send_proj(s).start()
        lp[s] = proj[s, :, mine]

        def first(j, carry):
            left = proj[s]
            v = jnp.dot(left, win[:, tile(j)], preferred_element_type=f32)
            g = jax.nn.sigmoid(
                jnp.dot(left, win[:, tile(j, width)], preferred_element_type=f32)
            )
            val[s, :, tile(j)] = v
            gate[s, :, tile(j)] = g
            gated = v * g * pad[s]
            for m in range(group):
                gpad[s * group + m, EDGE : EDGE + length, tile(j)] = gated[
                    m * length : (m + 1) * length
                ]
            for m in range(group):
                for c in range(TILE // LANES):
                    cols = pl.ds(pl.multiple_of(j * TILE + c * LANES, LANES), LANES)
                    acc = jnp.zeros((length, LANES), f32)
                    for b in range(8):
                        rolled = gpad[s * group + m, b : b + length + 24, cols]
                        for a in range(4):
                            k = 8 * a + b - 1
                            if 0 <= k < kernel:
                                acc = acc + rolled[8 * a : 8 * a + length] * taps[k : k + 1, cols]
                    mid[m * length : (m + 1) * length, cols] = acc
            return carry

        lax.fori_loop(0, tiles, first, 0)
        normed2, inv2 = norm_stats(mid[...])
        nmid[s] = normed2
        inv_mid[s] = inv2
        scaled = normed2 * gain_mid[...]
        sw[s] = (scaled * jax.nn.sigmoid(scaled)).astype(bf16)
        send_sw(s).start()
        ls[s] = sw[s, :, mine]

        @pl.when((sec <= 1) & (s == 0))
        def _():
            rest_of_weights()

        @pl.when(sec < sections - 1)
        def _():
            def second(j, carry):
                out = jnp.dot(sw[s], wout[:, tile(j)], preferred_element_type=f32)
                xout[s, :, tile(j)] = (xin[s, :, tile(j)].astype(f32) + out).astype(bf16)
                return carry

            lax.fori_loop(0, tiles, second, 0)
            send_forward(s).start()

        return carry

    lax.fori_loop(0, steps, forward, 0)

    nt = (((1,), (1,)), ((), ()))

    def backward(s, carry):
        @pl.when(sec == sections - 1)
        def _():
            right[s, :, pl.ds(2 * width, width)] = cotangent[s]

        @pl.when(sec < sections - 1)
        def _():
            send_backward(s).wait_recv()

        send_up(s).start()
        zero = jnp.zeros((rows, 1), f32)

        def first(j, sums):
            up = right[s, :, pl.ds(2 * width, width)]
            sg = lax.dot_general(up, wout[tile(j), :], nt, preferred_element_type=f32)
            nm = nmid[s, :, tile(j)]
            gb = gain_mid[:, tile(j)]
            scaled = nm * gb
            sig = jax.nn.sigmoid(scaled)
            scg = sg * (sig + scaled * sig * (1.0 - sig))
            small[1:2, tile(j)] += jnp.sum(scg * nm, axis=0, keepdims=True)
            z = scg * gb
            mid[:, tile(j)] = z
            return (
                sums[0] + jnp.sum(z, axis=-1, keepdims=True),
                sums[1] + jnp.sum(z * nm, axis=-1, keepdims=True),
            )

        s1, s2 = lax.fori_loop(0, tiles, first, (zero, zero))
        s1 = s1 * (1.0 / width)
        s2 = s2 * (1.0 / width)

        def second(j, carry):
            cols = pl.ds(pl.multiple_of(j * LANES, LANES), LANES)
            gate_cols = pl.ds(pl.multiple_of(width + j * LANES, LANES), LANES)
            cg_all = (mid[:, cols] - s1 - nmid[s, :, cols] * s2) * inv_mid[s]
            conv_grad[:, cols] = cg_all
            for m in range(group):
                span_m = slice(m * length, (m + 1) * length)
                cg = cg_all[span_m]
                cpad[m, EDGE : EDGE + length, :] = cg
                acc = jnp.zeros((length, LANES), f32)
                for b in range(8):
                    rolled = cpad[m, b : b + length + 24, :]
                    for a in range(4):
                        k = kernel - 1 - (8 * a + b - 1)
                        if 0 <= k < kernel:
                            acc = acc + rolled[8 * a : 8 * a + length] * taps[k : k + 1, cols]
                acc = acc * pad[s, span_m]
                g = gate[s, span_m, cols]
                vg = acc * g
                right[s, span_m, cols] = vg.astype(bf16)
                right[s, span_m, gate_cols] = (
                    acc * val[s, span_m, cols] * g * (1.0 - g)
                ).astype(bf16)
            return carry

        lax.fori_loop(0, width // LANES, second, 0)
        send_grad(s).start()

        def third(j, sums):
            pg = right[s, :, pl.ds(0, 2 * width)]
            ins = lax.dot_general(pg, win[tile(j), :], nt, preferred_element_type=f32)
            nv = nin[s, :, tile(j)]
            small[0:1, tile(j)] += jnp.sum(ins * nv, axis=0, keepdims=True)
            z = ins * gain_pre[:, tile(j)]
            mid[:, tile(j)] = z
            return (
                sums[0] + jnp.sum(z, axis=-1, keepdims=True),
                sums[1] + jnp.sum(z * nv, axis=-1, keepdims=True),
            )

        m1, m2 = lax.fori_loop(0, tiles, third, (zero, zero))
        m1 = m1 * (1.0 / width)
        m2 = m2 * (1.0 / width)
        up = right[s, :, pl.ds(2 * width, width)].astype(f32)
        ig[s] = (up + (mid[...] - m1 - nin[s] * m2) * inv_in[s]).astype(bf16)

        @pl.when(sec > 0)
        def _():
            send_backward(s).start()

        def fourth(j, carry):
            cols = pl.ds(pl.multiple_of(j * LANES, LANES), LANES)
            for m in range(group):
                cg = conv_grad[m * length : (m + 1) * length, cols]
                for b in range(8):
                    rolled = gpad[s * group + m, b : b + length + 24, cols]
                    for a in range(4):
                        k = 8 * a + b - 1
                        if 0 <= k < kernel:
                            term = cg * rolled[8 * a : 8 * a + length]
                            tg[k, :, cols] += jnp.sum(term.reshape(length // 8, 8, LANES), axis=0)
            return carry

        lax.fori_loop(0, width // LANES, fourth, 0)
        return carry

    lax.fori_loop(0, steps, backward, 0)

    small[8 : 8 + kernel] = jnp.sum(tg[...], axis=1)
    swap = remote(small, small_y, sy_s, sy_r, fsdp=other)
    swap.start()

    parts = 6 * tiles
    depth = half // 2

    def place(p):
        at = lax.rem(p // 2 + 2 * tiles, 3 * tiles)
        return pl.ds(pl.multiple_of(lax.rem(p, 2) * depth, 16), depth), tile(at)

    def to_inner(p):
        where = place(p)
        return remote(part.at[where], arrived.at[where], a_s.at[p], a_r.at[p], batch=inner)

    def across(p):
        where = place(p)
        return remote(part.at[where], total.at[where], c_s.at[p], c_r.at[p], batch=opposite)

    def to_outer(p):
        where = place(p)
        return remote(total.at[where], total.at[where], t_s.at[p], t_r.at[p], batch=outer)

    small_to_inner = remote(small_sum, small_a, a_s.at[parts], a_r.at[parts], batch=inner)
    small_across = remote(small_sum, small_b, c_s.at[parts], c_r.at[parts], batch=opposite)
    small_to_outer = remote(small_total, small_total, t_s.at[parts], t_r.at[parts], batch=outer)

    tn = (((0,), (0,)), ((), ()))

    def finish(p):
        where = place(p)
        across(p).wait_recv()
        across(p).wait_send()
        total[where] = (part[where].astype(f32) + total[where].astype(f32)).astype(bf16)
        to_outer(p).start()

    def terms(left_ref, first_tile, count):
        def one(order, carry):
            cols = tile(lax.rem(order + 2 * tiles, 3 * tiles))
            left = left_ref[...].reshape(2 * steps * rows, half)
            block = right[:, :, cols].reshape(2 * steps * rows, TILE)
            part[:, cols] = lax.dot_general(
                left, block, tn, preferred_element_type=f32
            ).astype(bf16)

            @pl.when(edge)
            def _():
                def send(p, carry):
                    @pl.when(p >= IN_FLIGHT)
                    def _():
                        to_inner(p - IN_FLIGHT).wait_send()

                    to_inner(p).start()
                    return carry

                lax.fori_loop(2 * order, 2 * order + 2, send, 0)

            @pl.when(jnp.logical_not(edge))
            def _():
                def meet(p, carry):
                    where = place(p)
                    to_inner(p).wait_recv()
                    part[where] = (
                        part[where].astype(f32) + arrived[where].astype(f32)
                    ).astype(bf16)
                    across(p).start()

                    @pl.when(p > 0)
                    def _():
                        finish(p - 1)

                    return carry

                lax.fori_loop(2 * order, 2 * order + 2, meet, 0)

            return carry

        lax.fori_loop(first_tile, first_tile + count, one, 0)

    def arrivals_out(s, carry):
        send_sw(s).wait_recv()
        send_up(s).wait_recv()
        return carry

    def arrivals_in(s, carry):
        send_proj(s).wait_recv()
        send_grad(s).wait_recv()
        return carry

    lax.fori_loop(0, steps, arrivals_out, 0)
    terms(ls, 0, tiles)
    lax.fori_loop(0, steps, arrivals_in, 0)
    swap.wait_recv()
    small_sum[...] = small[...] + small_y[...]

    @pl.when(edge)
    def _():
        small_to_inner.start()

    @pl.when(jnp.logical_not(edge))
    def _():
        small_to_inner.wait_recv()
        small_sum[...] = small_sum[...] + small_a[...]
        small_across.start()

    terms(lp, tiles, 2 * tiles)

    @pl.when(jnp.logical_not(edge))
    def _():
        small_across.wait_recv()
        small_across.wait_send()
        small_total[...] = small_sum[...] + small_b[...]
        small_to_outer.start()
        finish(parts - 1)

        def sent(p, carry):
            to_outer(p).wait_send()
            return carry

        lax.fori_loop(0, parts, sent, 0)
        small_to_outer.wait_send()

    @pl.when(edge)
    def _():
        def left_over(p, carry):
            to_inner(p).wait_send()
            return carry

        def done(p, carry):
            to_outer(p).wait_recv()
            return carry

        lax.fori_loop(parts - IN_FLIGHT, parts, left_over, 0)
        lax.fori_loop(0, parts, done, 0)
        small_to_inner.wait_send()
        small_to_outer.wait_recv()

    for i in range(all_pieces):
        if i + IN_FLIGHT >= all_pieces:
            over_y(i).wait_send()
        over_z(i).wait_send()
    swap.wait_send()

    def drained(s, carry):
        send_proj(s).wait_send()
        send_sw(s).wait_send()
        send_up(s).wait_send()
        send_grad(s).wait_send()

        @pl.when(sec < sections - 1)
        def _():
            send_forward(s).wait_send()

        @pl.when(sec > 0)
        def _():
            send_backward(s).wait_send()

        return carry

    lax.fori_loop(0, steps, drained, 0)


def fused(frames, cotangent, lengths, w_in, w_out, gain_pre, gain_mid, w_depth):
    micro_count, _, length, width = frames.shape
    kernel = w_depth.shape[1]
    group = GROUP
    steps = micro_count // group
    rows = group * length
    half = w_in.shape[1]
    scale = 1.0 / math.sqrt(micro_count * length * lax.axis_size("fsdp") * lax.axis_size("batch"))
    f32, bf16 = jnp.float32, jnp.bfloat16
    parts = 6 * (width // TILE)
    small_rows = 8 + -(-kernel // 8) * 8
    vmem = pl.BlockSpec(memory_space=pltpu.VMEM)
    hbm = pl.BlockSpec(memory_space=pl.ANY)
    smem = pl.BlockSpec(memory_space=pltpu.SMEM)

    def buf(*shape, dtype=f32):
        return pltpu.VMEM(shape, dtype)

    def sem(*shape):
        return pltpu.SemaphoreType.DMA(shape)

    ig, total, small = pl.pallas_call(
        functools.partial(pipeline_kernel, (steps, group, length, width, kernel)),
        out_shape=(
            jax.ShapeDtypeStruct((steps, rows, width), bf16),
            jax.ShapeDtypeStruct((half, 3 * width), bf16),
            jax.ShapeDtypeStruct((small_rows, width), f32),
        ),
        in_specs=[vmem, vmem, smem, hbm, hbm, vmem, vmem, vmem],
        out_specs=(vmem, vmem, vmem),
        scratch_shapes=[
            buf(width, 2 * width, dtype=bf16),
            buf(width, width, dtype=bf16),
            buf(steps, rows, width, dtype=bf16),
            buf(steps, rows, width, dtype=bf16),
            buf(steps, rows, width),
            buf(steps, rows, 1),
            buf(steps, rows, width, dtype=bf16),
            buf(steps, rows, width),
            buf(steps, rows, width),
            buf(micro_count, length + 2 * EDGE, width),
            buf(steps, rows, width),
            buf(steps, rows, 1),
            buf(steps, rows, width, dtype=bf16),
            buf(rows, width),
            buf(group, length + 2 * EDGE, LANES),
            buf(kernel, 8, width),
            buf(2 * steps, rows, half, dtype=bf16),
            buf(2 * steps, rows, half, dtype=bf16),
            buf(2 * steps, rows, 3 * width, dtype=bf16),
            buf(half, 3 * width, dtype=bf16),
            buf(half, 3 * width, dtype=bf16),
            buf(rows, width),
            buf(steps, rows, 1),
            buf(small_rows, width),
            buf(small_rows, width),
            buf(small_rows, width),
            buf(small_rows, width),
            buf(small_rows, width),
            *[sem(IN_PIECES + OUT_PIECES) for _ in range(4)],
            sem(2),
            pltpu.SemaphoreType.REGULAR,
            *[sem(steps) for _ in range(12)],
            pltpu.SemaphoreType.DMA,
            pltpu.SemaphoreType.DMA,
            *[sem(parts + 1) for _ in range(6)],
        ],
        compiler_params=pltpu.CompilerParams(
            collective_id=0, has_side_effects=True, vmem_limit_bytes=62 * 1024 * 1024
        ),
    )(
        frames.reshape(steps, rows, width),
        cotangent.reshape(steps, rows, width),
        lengths,
        w_in[0],
        w_out[0],
        gain_pre,
        gain_mid,
        w_depth[0],
    )
    return (
        ig.reshape(1, micro_count, 1, length, width),
        (scale * total[:, : 2 * width].astype(f32))[None],
        (scale * total[:, 2 * width :].astype(f32))[None],
        (scale * small[0])[None],
        (scale * small[1])[None],
        (scale * small[8 : 8 + kernel])[None],
    )


def solution(mesh):
    in_specs = (
        P(None, ("fsdp", "batch"), None, None),
        P(None, ("fsdp", "batch"), None, None),
        P(None, ("fsdp", "batch")),
        P("section", "fsdp", None),
        P("section", "fsdp", None),
        P("section", None),
        P("section", None),
        P("section", None, None),
    )
    out_specs = (
        P("section", None, ("fsdp", "batch"), None, None),
        P("section", "fsdp", None),
        P("section", "fsdp", None),
        P("section", None),
        P("section", None),
        P("section", None, None),
    )
    paired = mesh.shape["fsdp"] == 2 and mesh.shape["batch"] == 4
    body = fused if paired else local
    return jax.shard_map(body, mesh=mesh, in_specs=in_specs, out_specs=out_specs, check_vma=False)
```

```python
import functools
import math

import jax
import jax.numpy as jnp
from jax import lax
from jax.experimental import pallas as pl
from jax.experimental.pallas import tpu as pltpu
from jax.sharding import PartitionSpec as P

epsilon = 1e-05
GROUP = 2


def from_behind(x, axis, by):
    peers = lax.axis_size(axis)
    pairs = [(i, i + by) for i in range(peers) if 0 <= i + by < peers]
    return lax.ppermute(x, axis, pairs)


def layer_norm(values):
    mean_value = jnp.mean(values, axis=-1, keepdims=True)
    centred = values - mean_value
    inv_scale = lax.rsqrt(jnp.mean(centred * centred, axis=-1, keepdims=True) + epsilon)
    return (centred * inv_scale, inv_scale)


def norm_grad(upstream, normed, inv_scale):
    return (
        upstream
        - jnp.mean(upstream, axis=-1, keepdims=True)
        - normed * jnp.mean(upstream * normed, axis=-1, keepdims=True)
    ) * inv_scale


def project(left, right):
    batch_rows, length, inner = left.shape
    flat = jnp.dot(
        left.reshape(batch_rows * length, inner), right, preferred_element_type=jnp.float32
    )
    return flat.reshape(batch_rows, length, right.shape[1])


def project_back(left, right):
    batch_rows, length, inner = left.shape
    flat = lax.dot_general(
        left.reshape(batch_rows * length, inner),
        right,
        (((1,), (1,)), ((), ())),
        preferred_element_type=jnp.float32,
    )
    return flat.reshape(batch_rows, length, right.shape[0])


def depthwise(values, taps):
    kernel = taps.shape[0]
    half = kernel // 2
    length = values.shape[1]
    padded = jnp.pad(values, ((0, 0), (half, half), (0, 0)))
    total = padded[:, 0:length, :] * taps[0]
    for offset in range(1, kernel):
        total = total + padded[:, offset : offset + length, :] * taps[offset]
    return total


def section_forward(frames, w_in, w_out, gain_a, gain_b, taps, padding):
    model_width = frames.shape[-1]
    source = frames.astype(jnp.float32)
    normed_in, inv_in = layer_norm(source)
    projected = (normed_in * gain_a).astype(jnp.bfloat16)
    both = project(projected, w_in)
    glu_value = both[..., :model_width]
    glu_gate = jax.nn.sigmoid(both[..., model_width:])
    gated = glu_value * glu_gate * padding
    conv_out = depthwise(gated, taps)
    normed_mid, inv_mid = layer_norm(conv_out)
    scaled_mid = normed_mid * gain_b
    swished = (scaled_mid * jax.nn.sigmoid(scaled_mid)).astype(jnp.bfloat16)
    result = (source + project(swished, w_out)).astype(jnp.bfloat16)
    return (
        result,
        (
            normed_in,
            inv_in,
            projected,
            glu_value,
            glu_gate,
            gated,
            normed_mid,
            inv_mid,
            scaled_mid,
            swished,
        ),
    )


def section_backward(upstream, w_in, w_out, gain_a, gain_b, taps, padding, saved):
    (
        normed_in,
        inv_in,
        projected,
        glu_value,
        glu_gate,
        gated,
        normed_mid,
        inv_mid,
        scaled_mid,
        swished,
    ) = saved
    kernel = taps.shape[0]
    half = kernel // 2
    length = upstream.shape[1]
    swish_grad = project_back(upstream, w_out)
    sigmoid_mid = jax.nn.sigmoid(scaled_mid)
    scaled_grad = swish_grad * (sigmoid_mid + scaled_mid * sigmoid_mid * (1.0 - sigmoid_mid))
    gain_b_grad = jnp.sum(scaled_grad * normed_mid, axis=(0, 1))
    conv_grad = norm_grad(scaled_grad * gain_b, normed_mid, inv_mid)
    padded_in = jnp.pad(gated, ((0, 0), (half, half), (0, 0)))
    taps_grad = jnp.stack(
        [
            jnp.sum(conv_grad * padded_in[:, offset : offset + length, :], axis=(0, 1))
            for offset in range(kernel)
        ]
    )
    padded_grad = jnp.pad(conv_grad, ((0, 0), (half, half), (0, 0)))
    gated_grad = padded_grad[:, 2 * half : 2 * half + length, :] * taps[0]
    for offset in range(1, kernel):
        gated_grad = (
            gated_grad
            + padded_grad[:, 2 * half - offset : 2 * half - offset + length, :] * taps[offset]
        )
    gated_grad = gated_grad * padding
    value_grad = gated_grad * glu_gate
    gate_grad = gated_grad * glu_value * glu_gate * (1.0 - glu_gate)
    proj_grad = jnp.concatenate([value_grad, gate_grad], axis=-1).astype(jnp.bfloat16)
    input_side = project_back(proj_grad, w_in)
    gain_a_grad = jnp.sum(input_side * normed_in, axis=(0, 1))
    input_grad = (
        upstream.astype(jnp.float32) + norm_grad(input_side * gain_a, normed_in, inv_in)
    ).astype(jnp.bfloat16)
    return (input_grad, proj_grad, (gain_a_grad, gain_b_grad, taps_grad))


def saved_zeros(micro_count, frames_len, model_width):
    wide = (micro_count, 1, frames_len, model_width)
    narrow = (micro_count, 1, frames_len, 1)
    return (
        jnp.zeros(wide, jnp.float32),
        jnp.zeros(narrow, jnp.float32),
        jnp.zeros(wide, jnp.bfloat16),
        jnp.zeros(wide, jnp.float32),
        jnp.zeros(wide, jnp.float32),
        jnp.zeros(wide, jnp.float32),
        jnp.zeros(wide, jnp.float32),
        jnp.zeros(narrow, jnp.float32),
        jnp.zeros(wide, jnp.float32),
        jnp.zeros(wide, jnp.bfloat16),
    )


def put_slot(buffers, values, micro_slot):
    return jax.tree.map(
        lambda buffer, value: lax.dynamic_update_index_in_dim(buffer, value, micro_slot, 0),
        buffers,
        values,
    )


def take_slot(buffers, micro_slot):
    return jax.tree.map(
        lambda buffer: lax.dynamic_index_in_dim(buffer, micro_slot, 0, keepdims=False), buffers
    )


def local(frames, cotangent, lengths, w_in, w_out, gain_pre, gain_mid, w_depth):
    section_count = lax.axis_size("section")
    section_index = lax.axis_index("section")
    micro_count = frames.shape[0]
    frames_len = frames.shape[2]
    model_width = frames.shape[3]
    moments = micro_count + section_count - 1
    scale = 1.0 / math.sqrt(
        micro_count * frames_len * lax.axis_size("fsdp") * lax.axis_size("batch")
    )
    w_in_full, w_out_full = (
        lax.all_gather(w_in[0], "fsdp", axis=0, tiled=True),
        lax.all_gather(w_out[0], "fsdp", axis=0, tiled=True),
    )
    gain_a = gain_pre[0]
    gain_b = gain_mid[0]
    taps = w_depth[0]
    positions = jnp.arange(frames_len, dtype=jnp.int32)

    def frame_padding(micro_slot):
        return (positions < lengths[micro_slot, 0]).astype(jnp.float32).reshape(1, frames_len, 1)

    stored = saved_zeros(micro_count, frames_len, model_width)
    blank = jnp.zeros((1, frames_len, model_width), jnp.bfloat16)
    outgoing = blank
    for moment in range(moments):
        if moment > 0:
            incoming = from_behind(outgoing, "section", 1)
        else:
            incoming = blank
        if moment < micro_count:
            section_input = jnp.where(section_index == 0, frames[moment], incoming)
        else:
            section_input = incoming
        micro_index = moment - section_index
        active = (micro_index >= 0) & (micro_index < micro_count)
        micro_slot = jnp.clip(micro_index, 0, micro_count - 1)

        def advance(operands, micro_slot=micro_slot):
            current, buffers = operands
            result, saved = section_forward(
                current, w_in_full, w_out_full, gain_a, gain_b, taps, frame_padding(micro_slot)
            )
            return (result, put_slot(buffers, saved, micro_slot))

        def bypass(operands):
            return (jnp.zeros_like(operands[0]), operands[1])

        outgoing, stored = lax.cond(active, advance, bypass, (section_input, stored))
    row_buffers = (
        jnp.zeros((micro_count, frames_len, model_width), jnp.bfloat16),
        jnp.zeros((micro_count, frames_len, 2 * model_width), jnp.bfloat16),
        jnp.zeros((micro_count, frames_len, model_width), jnp.bfloat16),
        jnp.zeros((micro_count, frames_len, model_width), jnp.bfloat16),
        jnp.zeros((micro_count, frames_len, model_width), jnp.bfloat16),
    )
    small_sums = (
        jnp.zeros((model_width,), jnp.float32),
        jnp.zeros((model_width,), jnp.float32),
        jnp.zeros(taps.shape, jnp.float32),
    )
    returning = blank
    for moment in range(moments):
        if moment > 0:
            incoming = from_behind(returning, "section", -1)
        else:
            incoming = blank
        if moment < micro_count:
            upstream = jnp.where(section_index == section_count - 1, cotangent[moment], incoming)
        else:
            upstream = incoming
        micro_index = moment - (section_count - 1 - section_index)
        active = (micro_index >= 0) & (micro_index < micro_count)
        micro_slot = jnp.clip(micro_index, 0, micro_count - 1)

        def retreat(operands, micro_slot=micro_slot):
            current, buffers, totals = operands
            padding = frame_padding(micro_slot)
            saved = take_slot(stored, micro_slot)
            input_grad, proj_grad, minor_grads = section_backward(
                current, w_in_full, w_out_full, gain_a, gain_b, taps, padding, saved
            )
            row_values = (saved[2][0], proj_grad[0], saved[9][0], current[0], input_grad[0])
            buffers = put_slot(buffers, row_values, micro_slot)
            totals = tuple((total + extra for total, extra in zip(totals, minor_grads)))
            return (input_grad, buffers, totals)

        def hold(operands):
            return (jnp.zeros_like(operands[0]), operands[1], operands[2])

        returning, row_buffers, small_sums = lax.cond(
            active, retreat, hold, (upstream, row_buffers, small_sums)
        )
    total_rows = micro_count * frames_len
    proj_rows = row_buffers[0].reshape(total_rows, model_width)
    grad_rows = row_buffers[1].reshape(total_rows, 2 * model_width)
    swish_rows = row_buffers[2].reshape(total_rows, model_width)
    upstream_rows = row_buffers[3].reshape(total_rows, model_width)
    term_in = lax.dot_general(
        proj_rows, grad_rows, (((0,), (0,)), ((), ())), preferred_element_type=jnp.float32
    )
    term_out = lax.dot_general(
        swish_rows, upstream_rows, (((0,), (0,)), ((), ())), preferred_element_type=jnp.float32
    )
    rounded_in = lax.optimization_barrier(term_in.astype(jnp.bfloat16)).astype(jnp.float32)
    rounded_out = lax.optimization_barrier(term_out.astype(jnp.bfloat16)).astype(jnp.float32)
    shares = (
        lax.psum_scatter(
            rounded_in.astype(jnp.bfloat16), "fsdp", scatter_dimension=0, tiled=True
        ).astype(jnp.float32),
        lax.psum_scatter(
            rounded_out.astype(jnp.bfloat16), "fsdp", scatter_dimension=0, tiled=True
        ).astype(jnp.float32),
    )
    grad_in, grad_out = (
        lax.psum(shares[0].astype(jnp.bfloat16), "batch").astype(jnp.float32),
        lax.psum(shares[1].astype(jnp.bfloat16), "batch").astype(jnp.float32),
    )
    small_total = lax.psum((small_sums[0], small_sums[1], small_sums[2]), ("fsdp", "batch"))
    input_grads = row_buffers[4].reshape(1, micro_count, 1, frames_len, model_width)
    return (
        input_grads,
        (scale * grad_in)[None],
        (scale * grad_out)[None],
        (scale * small_total[0])[None],
        (scale * small_total[1])[None],
        (scale * small_total[2])[None],
    )


TILE = 256
LANES = 128
EDGE = 16
IN_PIECES = 8
OUT_PIECES = 4
IN_FLIGHT = 3


def pipeline_kernel(
    dims,
    frames,
    cotangent,
    lengths,
    w_in,
    w_out,
    gain_pre,
    gain_mid,
    taps,
    ig,
    total,
    small_total,
    win,
    wout,
    xin,
    xout,
    nin,
    inv_in,
    proj,
    val,
    gate,
    gpad,
    nmid,
    inv_mid,
    sw,
    mid,
    cpad,
    tg,
    lp,
    ls,
    right,
    part,
    arrived,
    conv_grad,
    pad,
    small,
    small_y,
    small_sum,
    small_a,
    small_b,
    w_ys,
    w_yr,
    w_zs,
    w_zr,
    w_loc,
    turn,
    f_s,
    f_r,
    b_s,
    b_r,
    yp_s,
    yp_r,
    ysw_s,
    ysw_r,
    yu_s,
    yu_r,
    yg_s,
    yg_r,
    sy_s,
    sy_r,
    a_s,
    a_r,
    c_s,
    c_r,
    t_s,
    t_r,
):
    steps, group, length, width, kernel = dims
    rows = group * length
    tiles = width // TILE
    half = width // 2
    f32, bf16 = jnp.float32, jnp.bfloat16
    sections = lax.axis_size("section")
    sec = lax.axis_index("section")
    fs = lax.axis_index("fsdp")
    ba = lax.axis_index("batch")
    other = 1 - fs
    mate = ba + 1 - 2 * lax.rem(ba, 2)
    parity = lax.rem(ba, 2)
    edge = (ba == 0) | (ba == 3)
    inner = jnp.where(ba == 0, 1, 2)
    outer = jnp.where(ba == 1, 0, 3)
    opposite = 3 - ba

    def remote(src, dst, send, recv, **where):
        return pltpu.make_async_remote_copy(
            src_ref=src,
            dst_ref=dst,
            send_sem=send,
            recv_sem=recv,
            device_id=where,
            device_id_type=pl.DeviceIdType.MESH,
        )

    def tile(j, base=0):
        return pl.ds(pl.multiple_of(base + j * TILE, TILE), TILE)

    barrier = pltpu.get_barrier_semaphore()
    for where in (
        {"section": lax.rem(sec + 1, sections)},
        {"section": lax.rem(sec + sections - 1, sections)},
        {"fsdp": other},
        {"batch": lax.rem(ba + 1, 4)},
        {"batch": lax.rem(ba + 3, 4)},
    ):
        pl.semaphore_signal(barrier, inc=1, device_id=where, device_id_type=pl.DeviceIdType.MESH)
    pl.semaphore_wait(barrier, 5)

    pieces = [(w_in, win, half // 16, 2 * i) for i in range(IN_PIECES)]
    pieces += [(w_out, wout, half // 8, 2 * i) for i in range(OUT_PIECES)]

    def span(size, first, which, owner=None):
        begin = (first + which) * size
        if owner is not None:
            begin = owner * half + begin
        return pl.ds(pl.multiple_of(begin, 16), size)

    def over_y(i):
        src, dst, size, first = pieces[i]
        return remote(
            src.at[span(size, first, parity)],
            dst.at[span(size, first, parity, fs)],
            w_ys.at[i],
            w_yr.at[i],
            fsdp=other,
        )

    def over_z(i):
        _, dst, size, first = pieces[i]
        block = dst.at[span(size, first, parity, other)]
        return remote(block, block, w_zs.at[i], w_zr.at[i], batch=mate)

    own = pl.ds(pl.multiple_of(fs * half, 16), half)
    own_in = pltpu.make_async_copy(w_in, win.at[own], w_loc.at[0])
    own_out = pltpu.make_async_copy(w_out, wout.at[own], w_loc.at[1])
    own_in.start()
    own_out.start()

    gpad[...] = jnp.zeros_like(gpad)
    cpad[...] = jnp.zeros_like(cpad)
    tg[...] = jnp.zeros_like(tg)
    small[...] = jnp.zeros_like(small)
    frame = lax.broadcasted_iota(jnp.int32, (length, 1), 0)
    for m in range(steps * group):
        first_row = (m % group) * length
        pad[m // group, first_row : first_row + length] = jnp.where(
            frame < lengths[m, 0], 1.0, 0.0
        ).astype(f32)

    all_pieces = IN_PIECES + OUT_PIECES
    second_of_pair = lax.rem(sec, 2) == 1

    @pl.when(second_of_pair)
    def _():
        pl.semaphore_wait(turn, 1)

    for i in range(IN_FLIGHT):
        over_y(i).start()

    def pass_on(i):
        over_y(i).wait_recv()
        over_z(i).start()
        if i + IN_FLIGHT < all_pieces:
            over_y(i).wait_send()
            over_y(i + IN_FLIGHT).start()

    for i in range(IN_PIECES):
        pass_on(i)
    own_in.wait()
    for i in range(IN_PIECES):
        over_z(i).wait_recv()

    def rest_of_weights():
        for i in range(IN_PIECES, all_pieces):
            pass_on(i)

        @pl.when(jnp.logical_not(second_of_pair))
        def _():
            pl.semaphore_signal(
                turn,
                inc=1,
                device_id={"section": sec + 1},
                device_id_type=pl.DeviceIdType.MESH,
            )

        own_out.wait()
        for i in range(IN_PIECES, all_pieces):
            over_z(i).wait_recv()

    @pl.when(sec > 1)
    def _():
        rest_of_weights()

    mine = pl.ds(pl.multiple_of(fs * half, LANES), half)
    theirs = pl.ds(pl.multiple_of(other * half, LANES), half)

    def send_forward(s):
        return remote(xout.at[s], xin.at[s], f_s.at[s], f_r.at[s], section=lax.rem(sec + 1, sections))

    def send_backward(s):
        return remote(
            ig.at[s],
            right.at[s, :, pl.ds(2 * width, width)],
            b_s.at[s],
            b_r.at[s],
            section=lax.rem(sec + sections - 1, sections),
        )

    def send_proj(s):
        return remote(proj.at[s, :, theirs], lp.at[steps + s], yp_s.at[s], yp_r.at[s], fsdp=other)

    def send_sw(s):
        return remote(sw.at[s, :, theirs], ls.at[steps + s], ysw_s.at[s], ysw_r.at[s], fsdp=other)

    def send_up(s):
        cols = pl.ds(2 * width, width)
        return remote(
            right.at[s, :, cols], right.at[steps + s, :, cols], yu_s.at[s], yu_r.at[s], fsdp=other
        )

    def send_grad(s):
        cols = pl.ds(0, 2 * width)
        return remote(
            right.at[s, :, cols], right.at[steps + s, :, cols], yg_s.at[s], yg_r.at[s], fsdp=other
        )

    def norm_stats(values):
        mean_value = jnp.sum(values, axis=-1, keepdims=True) * (1.0 / width)
        centred = values - mean_value
        inv = lax.rsqrt(jnp.sum(centred * centred, axis=-1, keepdims=True) * (1.0 / width) + epsilon)
        return centred * inv, inv

    def forward(s, carry):
        @pl.when(sec == 0)
        def _():
            xin[s] = frames[s]

        @pl.when(sec > 0)
        def _():
            send_forward(s).wait_recv()

        normed, inv = norm_stats(xin[s].astype(f32))
        nin[s] = normed
        inv_in[s] = inv
        proj[s] = (normed * gain_pre[...]).astype(bf16)
        send_proj(s).start()
        lp[s] = proj[s, :, mine]

        def first(j, carry):
            left = proj[s]
            v = jnp.dot(left, win[:, tile(j)], preferred_element_type=f32)
            g = jax.nn.sigmoid(
                jnp.dot(left, win[:, tile(j, width)], preferred_element_type=f32)
            )
            val[s, :, tile(j)] = v
            gate[s, :, tile(j)] = g
            gated = v * g * pad[s]
            for m in range(group):
                gpad[s * group + m, EDGE : EDGE + length, tile(j)] = gated[
                    m * length : (m + 1) * length
                ]
            for m in range(group):
                for c in range(TILE // LANES):
                    cols = pl.ds(pl.multiple_of(j * TILE + c * LANES, LANES), LANES)
                    acc = jnp.zeros((length, LANES), f32)
                    for b in range(8):
                        rolled = gpad[s * group + m, b : b + length + 24, cols]
                        for a in range(4):
                            k = 8 * a + b - 1
                            if 0 <= k < kernel:
                                acc = acc + rolled[8 * a : 8 * a + length] * taps[k : k + 1, cols]
                    mid[m * length : (m + 1) * length, cols] = acc
            return carry

        lax.fori_loop(0, tiles, first, 0)
        normed2, inv2 = norm_stats(mid[...])
        nmid[s] = normed2
        inv_mid[s] = inv2
        scaled = normed2 * gain_mid[...]
        sw[s] = (scaled * jax.nn.sigmoid(scaled)).astype(bf16)
        send_sw(s).start()
        ls[s] = sw[s, :, mine]

        @pl.when((sec <= 1) & (s == 0))
        def _():
            rest_of_weights()

        @pl.when(sec < sections - 1)
        def _():
            def second(j, carry):
                out = jnp.dot(sw[s], wout[:, tile(j)], preferred_element_type=f32)
                xout[s, :, tile(j)] = (xin[s, :, tile(j)].astype(f32) + out).astype(bf16)
                return carry

            lax.fori_loop(0, tiles, second, 0)
            send_forward(s).start()

        return carry

    lax.fori_loop(0, steps, forward, 0)

    nt = (((1,), (1,)), ((), ()))

    def backward(s, carry):
        @pl.when(sec == sections - 1)
        def _():
            right[s, :, pl.ds(2 * width, width)] = cotangent[s]

        @pl.when(sec < sections - 1)
        def _():
            send_backward(s).wait_recv()

        send_up(s).start()
        zero = jnp.zeros((rows, 1), f32)

        def turned(weights, values):
            def one(j, carry):
                span_j = pl.ds(pl.multiple_of(j * half, LANES), half)
                product = lax.dot_general(
                    weights[span_j, :], values(), nt, preferred_element_type=f32
                )
                mid[:, span_j] = product.T
                return carry

            lax.fori_loop(0, 2, one, 0)

        turned(wout, lambda: right[s, :, pl.ds(2 * width, width)])

        def first(j, sums):
            sg = mid[:, tile(j)]
            nm = nmid[s, :, tile(j)]
            gb = gain_mid[:, tile(j)]
            scaled = nm * gb
            sig = jax.nn.sigmoid(scaled)
            scg = sg * (sig + scaled * sig * (1.0 - sig))
            small[1:2, tile(j)] += jnp.sum(scg * nm, axis=0, keepdims=True)
            z = scg * gb
            mid[:, tile(j)] = z
            return (
                sums[0] + jnp.sum(z, axis=-1, keepdims=True),
                sums[1] + jnp.sum(z * nm, axis=-1, keepdims=True),
            )

        s1, s2 = lax.fori_loop(0, tiles, first, (zero, zero))
        s1 = s1 * (1.0 / width)
        s2 = s2 * (1.0 / width)

        def second(j, carry):
            cols = pl.ds(pl.multiple_of(j * LANES, LANES), LANES)
            gate_cols = pl.ds(pl.multiple_of(width + j * LANES, LANES), LANES)
            cg_all = (mid[:, cols] - s1 - nmid[s, :, cols] * s2) * inv_mid[s]
            conv_grad[:, cols] = cg_all
            for m in range(group):
                span_m = slice(m * length, (m + 1) * length)
                cg = cg_all[span_m]
                cpad[m, EDGE : EDGE + length, :] = cg
                acc = jnp.zeros((length, LANES), f32)
                for b in range(8):
                    rolled = cpad[m, b : b + length + 24, :]
                    for a in range(4):
                        k = kernel - 1 - (8 * a + b - 1)
                        if 0 <= k < kernel:
                            acc = acc + rolled[8 * a : 8 * a + length] * taps[k : k + 1, cols]
                acc = acc * pad[s, span_m]
                g = gate[s, span_m, cols]
                vg = acc * g
                right[s, span_m, cols] = vg.astype(bf16)
                right[s, span_m, gate_cols] = (
                    acc * val[s, span_m, cols] * g * (1.0 - g)
                ).astype(bf16)
            return carry

        lax.fori_loop(0, width // LANES, second, 0)
        send_grad(s).start()

        turned(win, lambda: right[s, :, pl.ds(0, 2 * width)])

        def third(j, sums):
            ins = mid[:, tile(j)]
            nv = nin[s, :, tile(j)]
            small[0:1, tile(j)] += jnp.sum(ins * nv, axis=0, keepdims=True)
            z = ins * gain_pre[:, tile(j)]
            mid[:, tile(j)] = z
            return (
                sums[0] + jnp.sum(z, axis=-1, keepdims=True),
                sums[1] + jnp.sum(z * nv, axis=-1, keepdims=True),
            )

        m1, m2 = lax.fori_loop(0, tiles, third, (zero, zero))
        m1 = m1 * (1.0 / width)
        m2 = m2 * (1.0 / width)
        up = right[s, :, pl.ds(2 * width, width)].astype(f32)
        ig[s] = (up + (mid[...] - m1 - nin[s] * m2) * inv_in[s]).astype(bf16)

        @pl.when(sec > 0)
        def _():
            send_backward(s).start()

        def fourth(j, carry):
            cols = pl.ds(pl.multiple_of(j * LANES, LANES), LANES)
            for m in range(group):
                cg = conv_grad[m * length : (m + 1) * length, cols]
                for b in range(8):
                    rolled = gpad[s * group + m, b : b + length + 24, cols]
                    for a in range(4):
                        k = 8 * a + b - 1
                        if 0 <= k < kernel:
                            term = cg * rolled[8 * a : 8 * a + length]
                            tg[k, :, cols] += jnp.sum(term.reshape(length // 8, 8, LANES), axis=0)
            return carry

        lax.fori_loop(0, width // LANES, fourth, 0)
        return carry

    lax.fori_loop(0, steps, backward, 0)

    small[8 : 8 + kernel] = jnp.sum(tg[...], axis=1)
    swap = remote(small, small_y, sy_s, sy_r, fsdp=other)
    swap.start()

    parts = 6 * tiles
    depth = half // 2

    def place(p):
        at = lax.rem(p // 2 + 2 * tiles, 3 * tiles)
        return pl.ds(pl.multiple_of(lax.rem(p, 2) * depth, 16), depth), tile(at)

    def to_inner(p):
        where = place(p)
        return remote(part.at[where], arrived.at[where], a_s.at[p], a_r.at[p], batch=inner)

    def across(p):
        where = place(p)
        return remote(part.at[where], total.at[where], c_s.at[p], c_r.at[p], batch=opposite)

    def to_outer(p):
        where = place(p)
        return remote(total.at[where], total.at[where], t_s.at[p], t_r.at[p], batch=outer)

    small_to_inner = remote(small_sum, small_a, a_s.at[parts], a_r.at[parts], batch=inner)
    small_across = remote(small_sum, small_b, c_s.at[parts], c_r.at[parts], batch=opposite)
    small_to_outer = remote(small_total, small_total, t_s.at[parts], t_r.at[parts], batch=outer)

    tn = (((0,), (0,)), ((), ()))

    def finish(p):
        where = place(p)
        across(p).wait_recv()
        across(p).wait_send()
        total[where] = (part[where].astype(f32) + total[where].astype(f32)).astype(bf16)
        to_outer(p).start()

    def terms(left_ref, first_tile, count):
        def one(order, carry):
            cols = tile(lax.rem(order + 2 * tiles, 3 * tiles))
            left = left_ref[...].reshape(2 * steps * rows, half)
            block = right[:, :, cols].reshape(2 * steps * rows, TILE)
            part[:, cols] = lax.dot_general(
                left, block, tn, preferred_element_type=f32
            ).astype(bf16)

            @pl.when(edge)
            def _():
                def send(p, carry):
                    @pl.when(p >= IN_FLIGHT)
                    def _():
                        to_inner(p - IN_FLIGHT).wait_send()

                    to_inner(p).start()
                    return carry

                lax.fori_loop(2 * order, 2 * order + 2, send, 0)

            @pl.when(jnp.logical_not(edge))
            def _():
                def meet(p, carry):
                    where = place(p)
                    to_inner(p).wait_recv()
                    part[where] = (
                        part[where].astype(f32) + arrived[where].astype(f32)
                    ).astype(bf16)
                    across(p).start()

                    @pl.when(p > 0)
                    def _():
                        finish(p - 1)

                    return carry

                lax.fori_loop(2 * order, 2 * order + 2, meet, 0)

            return carry

        lax.fori_loop(first_tile, first_tile + count, one, 0)

    def arrivals_out(s, carry):
        send_sw(s).wait_recv()
        send_up(s).wait_recv()
        return carry

    def arrivals_in(s, carry):
        send_proj(s).wait_recv()
        send_grad(s).wait_recv()
        return carry

    lax.fori_loop(0, steps, arrivals_out, 0)
    terms(ls, 0, tiles)
    lax.fori_loop(0, steps, arrivals_in, 0)
    swap.wait_recv()
    small_sum[...] = small[...] + small_y[...]

    @pl.when(edge)
    def _():
        small_to_inner.start()

    @pl.when(jnp.logical_not(edge))
    def _():
        small_to_inner.wait_recv()
        small_sum[...] = small_sum[...] + small_a[...]
        small_across.start()

    terms(lp, tiles, 2 * tiles)

    @pl.when(jnp.logical_not(edge))
    def _():
        small_across.wait_recv()
        small_across.wait_send()
        small_total[...] = small_sum[...] + small_b[...]
        small_to_outer.start()
        finish(parts - 1)

        def sent(p, carry):
            to_outer(p).wait_send()
            return carry

        lax.fori_loop(0, parts, sent, 0)
        small_to_outer.wait_send()

    @pl.when(edge)
    def _():
        def left_over(p, carry):
            to_inner(p).wait_send()
            return carry

        def done(p, carry):
            to_outer(p).wait_recv()
            return carry

        lax.fori_loop(parts - IN_FLIGHT, parts, left_over, 0)
        lax.fori_loop(0, parts, done, 0)
        small_to_inner.wait_send()
        small_to_outer.wait_recv()

    for i in range(all_pieces):
        if i + IN_FLIGHT >= all_pieces:
            over_y(i).wait_send()
        over_z(i).wait_send()
    swap.wait_send()

    def drained(s, carry):
        send_proj(s).wait_send()
        send_sw(s).wait_send()
        send_up(s).wait_send()
        send_grad(s).wait_send()

        @pl.when(sec < sections - 1)
        def _():
            send_forward(s).wait_send()

        @pl.when(sec > 0)
        def _():
            send_backward(s).wait_send()

        return carry

    lax.fori_loop(0, steps, drained, 0)


def fused(frames, cotangent, lengths, w_in, w_out, gain_pre, gain_mid, w_depth):
    micro_count, _, length, width = frames.shape
    kernel = w_depth.shape[1]
    group = GROUP
    steps = micro_count // group
    rows = group * length
    half = w_in.shape[1]
    scale = 1.0 / math.sqrt(micro_count * length * lax.axis_size("fsdp") * lax.axis_size("batch"))
    f32, bf16 = jnp.float32, jnp.bfloat16
    parts = 6 * (width // TILE)
    small_rows = 8 + -(-kernel // 8) * 8
    vmem = pl.BlockSpec(memory_space=pltpu.VMEM)
    hbm = pl.BlockSpec(memory_space=pl.ANY)
    smem = pl.BlockSpec(memory_space=pltpu.SMEM)

    def buf(*shape, dtype=f32):
        return pltpu.VMEM(shape, dtype)

    def sem(*shape):
        return pltpu.SemaphoreType.DMA(shape)

    ig, total, small = pl.pallas_call(
        functools.partial(pipeline_kernel, (steps, group, length, width, kernel)),
        out_shape=(
            jax.ShapeDtypeStruct((steps, rows, width), bf16),
            jax.ShapeDtypeStruct((half, 3 * width), bf16),
            jax.ShapeDtypeStruct((small_rows, width), f32),
        ),
        in_specs=[vmem, vmem, smem, hbm, hbm, vmem, vmem, vmem],
        out_specs=(vmem, vmem, vmem),
        scratch_shapes=[
            buf(width, 2 * width, dtype=bf16),
            buf(width, width, dtype=bf16),
            buf(steps, rows, width, dtype=bf16),
            buf(steps, rows, width, dtype=bf16),
            buf(steps, rows, width),
            buf(steps, rows, 1),
            buf(steps, rows, width, dtype=bf16),
            buf(steps, rows, width),
            buf(steps, rows, width),
            buf(micro_count, length + 2 * EDGE, width),
            buf(steps, rows, width),
            buf(steps, rows, 1),
            buf(steps, rows, width, dtype=bf16),
            buf(rows, width),
            buf(group, length + 2 * EDGE, LANES),
            buf(kernel, 8, width),
            buf(2 * steps, rows, half, dtype=bf16),
            buf(2 * steps, rows, half, dtype=bf16),
            buf(2 * steps, rows, 3 * width, dtype=bf16),
            buf(half, 3 * width, dtype=bf16),
            buf(half, 3 * width, dtype=bf16),
            buf(rows, width),
            buf(steps, rows, 1),
            buf(small_rows, width),
            buf(small_rows, width),
            buf(small_rows, width),
            buf(small_rows, width),
            buf(small_rows, width),
            *[sem(IN_PIECES + OUT_PIECES) for _ in range(4)],
            sem(2),
            pltpu.SemaphoreType.REGULAR,
            *[sem(steps) for _ in range(12)],
            pltpu.SemaphoreType.DMA,
            pltpu.SemaphoreType.DMA,
            *[sem(parts + 1) for _ in range(6)],
        ],
        compiler_params=pltpu.CompilerParams(
            collective_id=0, has_side_effects=True, vmem_limit_bytes=62 * 1024 * 1024
        ),
    )(
        frames.reshape(steps, rows, width),
        cotangent.reshape(steps, rows, width),
        lengths,
        w_in[0],
        w_out[0],
        gain_pre,
        gain_mid,
        w_depth[0],
    )
    return (
        ig.reshape(1, micro_count, 1, length, width),
        (scale * total[:, : 2 * width].astype(f32))[None],
        (scale * total[:, 2 * width :].astype(f32))[None],
        (scale * small[0])[None],
        (scale * small[1])[None],
        (scale * small[8 : 8 + kernel])[None],
    )


def solution(mesh):
    in_specs = (
        P(None, ("fsdp", "batch"), None, None),
        P(None, ("fsdp", "batch"), None, None),
        P(None, ("fsdp", "batch")),
        P("section", "fsdp", None),
        P("section", "fsdp", None),
        P("section", None),
        P("section", None),
        P("section", None, None),
    )
    out_specs = (
        P("section", None, ("fsdp", "batch"), None, None),
        P("section", "fsdp", None),
        P("section", "fsdp", None),
        P("section", None),
        P("section", None),
        P("section", None, None),
    )
    paired = mesh.shape["fsdp"] == 2 and mesh.shape["batch"] == 4
    body = fused if paired else local
    return jax.shard_map(body, mesh=mesh, in_specs=in_specs, out_specs=out_specs, check_vma=False)
```
